512 devices in a mesh: dp: 4 (over z_hi, core), ctx: 128 (over y, x, z_lo).
Axes of the slice: x: 4, y: 8, z: 8 (z_hi: 2, z_lo: 4; z = z_hi * 4 + z_lo), core: 2. Of those that a mesh axis runs over, the one named last changes fastest.
Arguments:
- queries: bfloat16 [4, 16384, 384], P('dp', 'ctx'), may hold values from -6 to 6
- keys: bfloat16 [4, 16384, 384], P('dp', 'ctx'), may hold values from -6 to 6
- values: bfloat16 [4, 16384, 384], P('dp', 'ctx'), may hold values from -6 to 6
- filter_taps: bfloat16 [16384, 384], P('ctx'), may hold values from -6 to 6
- cotangent: bfloat16 [4, 16384, 384], P('dp', 'ctx'), may hold values from -6 to 6
Outputs:
- gated: bfloat16 [4, 16384, 384], P('dp', 'ctx')
- grad_queries: bfloat16 [4, 16384, 384], P('dp', 'ctx')
- grad_keys: bfloat16 [4, 16384, 384], P('dp', 'ctx')
- grad_values: bfloat16 [4, 16384, 384], P('dp', 'ctx')
- filter_grad: float32 [16384, 384], P('ctx')
The draws below stay inside these ranges and needn't reach their ends.
All inputs are finite; a program needn't handle non-finite values.
Results may differ from the reference program's by a relative error of at most 0.015.
Values may be sent and summed in bfloat16 or wider, within the bound.
A program may use at most 64 MiB of HBM per device.

```python
import math
import jax
import jax.numpy as jnp
from jax import lax

CH = 384
SEQ = 16384
BATCH = 4


def block_levels(rng, extent, pieces, low, top_value):
    level, own = 1.0, jax.random.fold_in(rng, 6)
    for position, parts in pieces:
        steps = jnp.exp(jax.random.uniform(jax.random.fold_in(own, position), (parts,), jnp.float32, low / len(pieces), top_value / len(pieces)))
        level = level * jnp.repeat(steps, extent[position] // parts).reshape([-1 if axis == position else 1 for axis in range(len(extent))])
    return level


def gaussian(rng, extent, scale, bound, cuts=(), held_as=jnp.bfloat16):
    array = jax.random.normal(rng, extent, jnp.float32) * scale
    if len(cuts) > 0:
        array = block_levels(rng, extent, cuts, -0.22, 0.18) * array
    return jnp.clip(array, min=-bound, max=bound).astype(held_as)


def setup_inputs(seed: int = 0) -> dict:
    streams_of = jax.random.split(jax.random.key(seed), 6)
    return {
        "queries": gaussian(streams_of[0], (BATCH, SEQ, CH), 1.0, 6.0, ((0, 4), (1, 128))),
        "keys": gaussian(streams_of[1], (BATCH, SEQ, CH), 1.0, 6.0, ((0, 4), (1, 128))),
        "values": gaussian(streams_of[2], (BATCH, SEQ, CH), 1.0, 6.0, ((0, 4), (1, 128))),
        "filter_taps": gaussian(streams_of[3], (SEQ, CH), 1.0, 6.0, ((0, 128),)),
        "cotangent": gaussian(streams_of[4], (BATCH, SEQ, CH), 1.0, 6.0, ((0, 4), (1, 128))),
    }


def reference(queries, keys, values, filter_taps, cotangent):
    length = 2 * SEQ
    factor = 1.0 / math.sqrt(SEQ)
    filter_spectrum = jnp.fft.rfft(filter_taps.astype(jnp.float32), n=length, axis=0) * factor

    def one_sequence(inputs):
        query_rows = inputs[0].astype(jnp.float32)
        key_rows = inputs[1].astype(jnp.float32)
        value_rows = inputs[2].astype(jnp.float32)
        grad_rows = inputs[3].astype(jnp.float32)
        mixed = lax.optimization_barrier((key_rows * value_rows).astype(jnp.bfloat16)).astype(jnp.float32)
        mixed_spectrum = jnp.fft.rfft(mixed, n=length, axis=0)
        conv = jnp.fft.irfft(mixed_spectrum * filter_spectrum, n=length, axis=0)[:SEQ]
        gated = (query_rows * conv).astype(jnp.bfloat16)
        grad_queries = (grad_rows * conv).astype(jnp.bfloat16)
        grad_conv = lax.optimization_barrier((grad_rows * query_rows).astype(jnp.bfloat16)).astype(jnp.float32)
        grad_spectrum = jnp.fft.rfft(grad_conv, n=length, axis=0)
        grad_mixed = jnp.fft.irfft(grad_spectrum * jnp.conj(filter_spectrum), n=length, axis=0)[:SEQ]
        grad_keys = (grad_mixed * value_rows).astype(jnp.bfloat16)
        grad_values = (grad_mixed * key_rows).astype(jnp.bfloat16)
        taps_part = jnp.fft.irfft(grad_spectrum * jnp.conj(mixed_spectrum), n=length, axis=0)[:SEQ]
        return (gated, grad_queries, grad_keys, grad_values, taps_part)
    results = lax.map(one_sequence, (queries, keys, values, cotangent))
    filter_grad = lax.optimization_barrier(jnp.sum(results[4], axis=0)) * factor
    return (results[0], results[1], results[2], results[3], filter_grad)
```

```python
import functools

import jax
import jax.numpy as jnp
import numpy as np
from jax import lax
from jax.experimental import pallas as pl
from jax.experimental.pallas import tpu as pltpu
from jax.sharding import PartitionSpec as P

MESH = pl.DeviceIdType.MESH
BF16 = jnp.bfloat16
F32 = jnp.float32


def dot(left, right, contract=(1, 0)):
    dims = (((contract[0],), (contract[1],)), ((), ()))
    return lax.dot_general(left, right, dims, preferred_element_type=F32)


def constant_tables(group, rows):
    total = group * rows
    outer = np.arange(group)
    inner = np.arange(rows)
    angle_outer = 2 * np.pi * np.outer(outer + 0.25, outer) / group
    angle_twist = 2 * np.pi * np.outer(outer + 0.25, inner) / total
    angle_inner = 2 * np.pi * np.outer(inner, inner) / rows
    cos_outer, sin_outer = np.cos(angle_outer), np.sin(angle_outer)
    forward = np.zeros((2, 2, group, group, 2))
    inverse = np.zeros((group, 2, 2, 2, group))
    scale = 1.0 / (total * np.sqrt(total))
    for slot in range(2):
        forward[slot, 0, :, :, slot] = cos_outer
        forward[slot, 1, :, :, slot] = -sin_outer
        inverse[:, slot, slot, 0, :] = cos_outer.T * scale
        inverse[:, slot, slot, 1, :] = -sin_outer.T * scale
    cos_inner, sin_inner = np.cos(angle_inner), np.sin(angle_inner)
    inner_forward = np.block([[cos_inner, -sin_inner], [sin_inner, cos_inner]])
    inner_inverse = np.block([[cos_inner, sin_inner], [-sin_inner, cos_inner]])
    pick = np.zeros((group, 2, 2, group))
    for slot in range(2):
        pick[outer, slot, slot, outer] = 1.0
    return (
        jnp.asarray(forward.reshape(4 * group, 2 * group), BF16),
        jnp.asarray(inverse.reshape(2 * group, 4 * group), BF16),
        jnp.asarray(inner_forward, BF16),
        jnp.asarray(inner_inverse, BF16),
        jnp.asarray(pick.reshape(2 * group, 2 * group), BF16),
        jnp.asarray(np.cos(angle_twist), F32),
        jnp.asarray(np.sin(angle_twist), F32),
    )


def kernel(
    group,
    parts,
    queries,
    keys,
    values,
    taps,
    cotangent,
    forward_hbm,
    inverse_hbm,
    inner_forward_hbm,
    inner_inverse_hbm,
    pick_hbm,
    twist_cos_hbm,
    twist_sin_hbm,
    gated,
    grad_queries,
    grad_keys,
    grad_values,
    filter_grad,
    q_buf,
    k_buf,
    v_buf,
    t_buf,
    c_buf,
    forward,
    inverse,
    inner_forward,
    inner_inverse,
    pick,
    twist_cos,
    twist_sin,
    send_pair,
    recv_pair,
    send_taps,
    recv_taps,
    send_back,
    recv_back,
    send_filter,
    sum_filter,
    recv_filter,
    recv_parts,
    turned,
    spectrum,
    product,
    untwisted,
    in_sem,
    table_sem,
    copy_sem,
):
    me = lax.axis_index("ctx")
    part = lax.axis_index("dp")
    lanes = queries.shape[1] // group
    rows = queries.shape[0]

    loads = [
        pltpu.make_async_copy(source, target, in_sem.at[index])
        for index, (source, target) in enumerate(
            [(keys, k_buf), (values, v_buf), (queries, q_buf), (cotangent, c_buf), (taps, t_buf), (pick_hbm, pick)]
        )
    ]
    tables = [
        pltpu.make_async_copy(source, target, table_sem.at[index])
        for index, (source, target) in enumerate(
            [
                (forward_hbm, forward),
                (twist_cos_hbm, twist_cos),
                (twist_sin_hbm, twist_sin),
                (inner_forward_hbm, inner_forward),
                (inner_inverse_hbm, inner_inverse),
                (inverse_hbm, inverse),
            ]
        )
    ]
    for load in loads + tables:
        load.start()

    barrier = pltpu.get_barrier_semaphore()

    @pl.loop(1, group)
    def _(step):
        pl.semaphore_signal(
            barrier, inc=1, device_id=(part, lax.rem(me + step, group)), device_id_type=MESH
        )

    for step in range(1, parts):
        pl.semaphore_signal(
            barrier, inc=1, device_id=(lax.rem(part + step, parts), me), device_id_type=MESH
        )

    for load in loads:
        load.wait()
    mixed = (k_buf[...].astype(F32) * v_buf[...].astype(F32)).astype(BF16)
    grad_conv = (c_buf[...].astype(F32) * q_buf[...].astype(F32)).astype(BF16)
    spread = pick[...]

    def block(array, index):
        return array[:, index * group : (index + 1) * group]

    pairs = jnp.concatenate(
        [jnp.concatenate([block(mixed, i), block(grad_conv, i)], axis=1) for i in range(lanes)], axis=0
    )
    send_pair[...] = dot(spread, pairs, (1, 1)).astype(BF16).reshape(send_pair.shape)
    tap_rows = t_buf[...]
    tap_pairs = jnp.concatenate(
        [
            jnp.concatenate([block(tap_rows, 0), block(tap_rows, 1)], axis=1),
            jnp.concatenate([block(tap_rows, 2), jnp.zeros((rows, group), BF16)], axis=1),
        ],
        axis=0,
    )
    send_taps[...] = dot(spread, tap_pairs, (1, 1)).astype(BF16).reshape(send_taps.shape)
    recv_pair[me] = send_pair[me]
    recv_taps[me] = send_taps[me]

    pl.semaphore_wait(barrier, group - 1 + parts - 1)

    def exchange(source, target, index):
        @pl.loop(1, group)
        def _(step):
            peer = lax.rem(me + step, group)
            pltpu.make_async_remote_copy(
                src_ref=source.at[peer],
                dst_ref=target.at[me],
                send_sem=copy_sem.at[index, 0],
                recv_sem=copy_sem.at[index, 1],
                device_id=(part, peer),
                device_id_type=MESH,
            ).start()

    def arrived(buffer, index, count, side):
        some = buffer.at[pl.ds(0, count)]
        pltpu.make_async_copy(some, some, copy_sem.at[index, side]).wait()

    exchange(send_pair, recv_pair, 0)
    exchange(send_taps, recv_taps, 1)

    for table in tables:
        table.wait()

    def twist(real_part, imag_part, slot):
        rows_here = pl.ds(slot * group, group)
        cosines, sines = twist_cos[...], twist_sin[...]
        turned[rows_here, pl.ds(0, rows)] = (real_part * cosines + imag_part * sines).astype(BF16)
        turned[rows_here, pl.ds(rows, rows)] = (imag_part * cosines - real_part * sines).astype(BF16)

    def stage_forward(buffer, slots, first):
        partial = dot(forward[...], buffer[...].reshape(2 * group, buffer.shape[2]))
        for offset, (r, j) in enumerate(slots):
            real_part = partial[2 * r * group : (2 * r + 1) * group, j * rows : (j + 1) * rows]
            imag_part = partial[(2 * r + 1) * group : (2 * r + 2) * group, j * rows : (j + 1) * rows]
            twist(real_part, imag_part, first + offset)
        here = pl.ds(first * group, len(slots) * group)
        spectrum[here, :] = dot(turned[here, :], inner_forward[...])

    def halves(slot):
        here = pl.ds(slot * group, group)
        return spectrum[here, pl.ds(0, rows)], spectrum[here, pl.ds(rows, rows)]

    def multiply(left, right, conjugate, slot):
        left_real, left_imag = halves(left)
        right_real, right_imag = halves(right)
        if conjugate:
            right_imag = -right_imag
        here = pl.ds(slot * group, group)
        product[here, pl.ds(0, rows)] = (left_real * right_real - left_imag * right_imag).astype(BF16)
        product[here, pl.ds(rows, rows)] = (left_real * right_imag + left_imag * right_real).astype(BF16)

    def stage_inverse(slots, first, target):
        here = pl.ds(first * group, len(slots) * group)
        back = dot(product[here, :], inner_inverse[...])
        cosines, sines = twist_cos[...], twist_sin[...]
        for offset, (r, j) in enumerate(slots):
            real_part = back[offset * group : (offset + 1) * group, :rows]
            imag_part = back[offset * group : (offset + 1) * group, rows:]
            across = pl.ds(j * rows, rows)
            untwisted[pl.ds(2 * r * group, group), across] = (real_part * cosines - imag_part * sines).astype(BF16)
            untwisted[pl.ds((2 * r + 1) * group, group), across] = (real_part * sines + imag_part * cosines).astype(BF16)
        width = target.shape[2]
        target[...] = dot(inverse[...], untwisted[:, pl.ds(0, width)]).astype(BF16).reshape(target.shape)

    pair_slots = [(r, j) for r in range(2) for j in range(lanes)]
    tap_slots = [(0, 0), (1, 0), (0, 1)]

    arrived(recv_pair, 0, group - 1, 1)
    stage_forward(recv_pair, pair_slots, 0)
    for i in range(lanes):
        multiply(lanes + i, i, True, i)
    untwisted[pl.ds(2 * group, 2 * group), pl.ds(rows, rows)] = jnp.zeros((2 * group, rows), BF16)
    stage_inverse(tap_slots, 0, send_filter)
    share = group // parts

    def to_parts(source, target, index):
        for step in range(1, parts):
            peer = lax.rem(part + step, parts)
            pltpu.make_async_remote_copy(
                src_ref=source(peer),
                dst_ref=target,
                send_sem=copy_sem.at[index, 0],
                recv_sem=copy_sem.at[index, 1],
                device_id=(peer, me),
                device_id_type=MESH,
            ).start()

    to_parts(lambda peer: send_filter.at[pl.ds(peer * share, share)], recv_parts.at[part], 4)

    arrived(recv_taps, 1, group - 1, 1)
    stage_forward(recv_taps, tap_slots, 2 * lanes)
    for i in range(lanes):
        multiply(i, 2 * lanes + i, False, i)
        multiply(lanes + i, 2 * lanes + i, True, lanes + i)
    stage_inverse(pair_slots, 0, send_back)
    exchange(send_back, recv_back, 2)
    recv_back[me] = send_back[me]

    arrived(recv_parts, 4, parts - 1, 1)
    total = send_filter[pl.ds(part * share, share)].astype(F32)
    for step in range(1, parts):
        total = total + recv_parts[lax.rem(part + step, parts)].astype(F32)
    mine = sum_filter.at[pl.ds(part * share, share)]
    mine[...] = total.astype(BF16)
    to_parts(lambda peer: mine, mine, 5)
    arrived(sum_filter, 5, (parts - 1) * share, 1)
    exchange(sum_filter, recv_filter, 3)
    recv_filter[me] = sum_filter[me]

    arrived(recv_back, 2, group - 1, 1)
    flat = recv_back[...].reshape(2 * group, lanes * rows)
    for i in range(lanes):
        both = dot(flat[:, i * rows : (i + 1) * rows], spread, (0, 0))
        conv, grad_mixed = both[:, :group], both[:, group:]
        here = pl.ds(i * group, group)
        gated[:, here] = (q_buf[:, here].astype(F32) * conv).astype(BF16)
        grad_queries[:, here] = (c_buf[:, here].astype(F32) * conv).astype(BF16)
        grad_keys[:, here] = (v_buf[:, here].astype(F32) * grad_mixed).astype(BF16)
        grad_values[:, here] = (k_buf[:, here].astype(F32) * grad_mixed).astype(BF16)
    arrived(recv_filter, 3, group - 1, 1)
    flat = recv_filter[...].reshape(2 * group, 2 * rows)
    for r, j in tap_slots:
        if r == 0:
            both = dot(flat[:, j * rows : (j + 1) * rows], spread, (0, 0))
        filter_grad[:, pl.ds((2 * j + r) * group, group)] = both[:, r * group : (r + 1) * group]

    for index, buffer in enumerate([send_pair, send_taps, send_back, sum_filter]):
        arrived(buffer, index, group - 1, 0)
    arrived(recv_parts, 4, parts - 1, 0)
    arrived(sum_filter, 5, (parts - 1) * share, 0)


def shards(group, parts, queries, keys, values, filter_taps, cotangent):
    rows, channels = filter_taps.shape
    lanes = channels // group
    tables = constant_tables(group, rows)
    share = group // parts
    vmem = pltpu.VMEM
    local = (rows, channels)
    pair = (group, 2, lanes * rows)
    single = (group, 2, 2 * rows)
    outs = pl.pallas_call(
        functools.partial(kernel, group, parts),
        out_shape=[jax.ShapeDtypeStruct(local, BF16)] * 4 + [jax.ShapeDtypeStruct(local, F32)],
        in_specs=[pl.BlockSpec(memory_space=pl.ANY)] * 12,
        out_specs=[pl.BlockSpec(memory_space=vmem)] * 5,
        scratch_shapes=[vmem(local, BF16)] * 5
        + [vmem(table.shape, table.dtype) for table in tables]
        + [vmem(pair, BF16)] * 2
        + [vmem(single, BF16)] * 2
        + [vmem(pair, BF16)] * 2
        + [vmem(single, BF16)] * 3
        + [
            vmem((parts, share, 2, 2 * rows), BF16),
            vmem((3 * lanes * group, 2 * rows), BF16),
            vmem((3 * lanes * group, 2 * rows), F32),
            vmem((2 * lanes * group, 2 * rows), BF16),
            vmem((4 * group, lanes * rows), BF16),
            pltpu.SemaphoreType.DMA((6,)),
            pltpu.SemaphoreType.DMA((6,)),
            pltpu.SemaphoreType.DMA((6, 2)),
        ],
        compiler_params=pltpu.CompilerParams(
            collective_id=0, has_side_effects=True, vmem_limit_bytes=56 << 20
        ),
    )(queries[0], keys[0], values[0], filter_taps, cotangent[0], *tables)
    return tuple(out[None] for out in outs[:4]) + (outs[4],)


def solution(mesh):
    spec = P("dp", "ctx", None)
    return jax.shard_map(
        functools.partial(shards, mesh.shape["ctx"], mesh.shape["dp"]),
        mesh=mesh,
        in_specs=(spec, spec, spec, P("ctx", None), spec),
        out_specs=(spec, spec, spec, spec, P("ctx", None)),
        check_vma=False,
    )
```

```python
import functools

import jax
import jax.numpy as jnp
import numpy as np
from jax import lax
from jax.experimental import pallas as pl
from jax.experimental.pallas import tpu as pltpu
from jax.sharding import PartitionSpec as P

MESH = pl.DeviceIdType.MESH
BF16 = jnp.bfloat16
F32 = jnp.float32


def dot(left, right, contract=(1, 0)):
    dims = (((contract[0],), (contract[1],)), ((), ()))
    return lax.dot_general(left, right, dims, preferred_element_type=F32)


def constant_tables(group, rows):
    total = group * rows
    outer = np.arange(group)
    inner = np.arange(rows)
    angle_outer = 2 * np.pi * np.outer(outer + 0.25, outer) / group
    angle_twist = 2 * np.pi * np.outer(outer + 0.25, inner) / total
    angle_inner = 2 * np.pi * np.outer(inner, inner) / rows
    cos_outer, sin_outer = np.cos(angle_outer), np.sin(angle_outer)
    forward = np.zeros((2, 2, group, group, 2))
    inverse = np.zeros((group, 2, 2, 2, group))
    scale = 1.0 / (total * np.sqrt(total))
    for slot in range(2):
        forward[slot, 0, :, :, slot] = cos_outer
        forward[slot, 1, :, :, slot] = -sin_outer
        inverse[:, slot, slot, 0, :] = cos_outer.T * scale
        inverse[:, slot, slot, 1, :] = -sin_outer.T * scale
    cos_inner, sin_inner = np.cos(angle_inner), np.sin(angle_inner)
    inner_forward = np.block([[cos_inner, -sin_inner], [sin_inner, cos_inner]])
    inner_inverse = np.block([[cos_inner, sin_inner], [-sin_inner, cos_inner]])
    pick = np.zeros((group, 2, 2, group))
    for slot in range(2):
        pick[outer, slot, slot, outer] = 1.0
    return (
        jnp.asarray(forward.reshape(4 * group, 2 * group), BF16),
        jnp.asarray(inverse.reshape(2 * group, 4 * group), BF16),
        jnp.asarray(inner_forward, BF16),
        jnp.asarray(inner_inverse, BF16),
        jnp.asarray(pick.reshape(2 * group, 2 * group), BF16),
        jnp.asarray(np.cos(angle_twist), F32),
        jnp.asarray(np.sin(angle_twist), F32),
    )


def kernel(
    group,
    parts,
    queries,
    keys,
    values,
    taps,
    cotangent,
    forward_hbm,
    inverse_hbm,
    inner_forward_hbm,
    inner_inverse_hbm,
    pick_hbm,
    twist_cos_hbm,
    twist_sin_hbm,
    recv_back,
    all_filter,
    q_buf,
    k_buf,
    v_buf,
    t_buf,
    c_buf,
    forward,
    inverse,
    inner_forward,
    inner_inverse,
    pick,
    twist_cos,
    twist_sin,
    send_pair,
    recv_pair,
    send_taps,
    recv_taps,
    send_back,
    send_filter,
    part_filter,
    sum_filter,
    recv_filter,
    turned,
    spectrum,
    product,
    untwisted,
    in_sem,
    table_sem,
    copy_sem,
    core_sem,
    ready_sem,
):
    me = lax.axis_index("ctx")
    part = lax.axis_index("dp")
    core = lax.rem(part, 2)
    pair = part // 2
    other = pair * 2 + 1 - core
    half = group // 2
    my_half = me // half
    lanes = queries.shape[1] // group
    rows = queries.shape[0]

    loads = [
        pltpu.make_async_copy(source, target, in_sem.at[index])
        for index, (source, target) in enumerate(
            [(keys, k_buf), (values, v_buf), (queries, q_buf), (cotangent, c_buf), (taps, t_buf), (pick_hbm, pick)]
        )
    ]
    tables = [
        pltpu.make_async_copy(source, target, table_sem.at[index])
        for index, (source, target) in enumerate(
            [
                (forward_hbm, forward),
                (twist_cos_hbm, twist_cos),
                (twist_sin_hbm, twist_sin),
                (inner_forward_hbm, inner_forward),
                (inner_inverse_hbm, inner_inverse),
                (inverse_hbm, inverse),
            ]
        )
    ]
    for load in loads + tables:
        load.start()

    barrier = pltpu.get_barrier_semaphore()

    @pl.loop(1, group)
    def _(step):
        pl.semaphore_signal(
            barrier, inc=1, device_id=(part, lax.rem(me + step, group)), device_id_type=MESH
        )

    for step in range(1, parts):
        pl.semaphore_signal(
            barrier, inc=1, device_id=(lax.rem(part + step, parts), me), device_id_type=MESH
        )

    for load in loads:
        load.wait()
    mixed = (k_buf[...].astype(F32) * v_buf[...].astype(F32)).astype(BF16)
    grad_conv = (c_buf[...].astype(F32) * q_buf[...].astype(F32)).astype(BF16)
    spread = pick[...]

    def block(array, index):
        return array[:, index * group : (index + 1) * group]

    pairs = jnp.concatenate(
        [jnp.concatenate([block(mixed, i), block(grad_conv, i)], axis=1) for i in range(lanes)], axis=0
    )
    send_pair[...] = dot(spread, pairs, (1, 1)).astype(BF16).reshape(send_pair.shape)
    tap_rows = t_buf[...]
    tap_pairs = jnp.concatenate(
        [
            jnp.concatenate([block(tap_rows, 0), block(tap_rows, 1)], axis=1),
            jnp.concatenate([block(tap_rows, 2), jnp.zeros((rows, group), BF16)], axis=1),
        ],
        axis=0,
    )
    send_taps[...] = dot(spread, tap_pairs, (1, 1)).astype(BF16).reshape(send_taps.shape)
    recv_pair[me] = send_pair[me]

    pl.semaphore_wait(barrier, group - 1 + parts - 1)
    for step in range(1, parts):
        pl.semaphore_signal(
            ready_sem.at[step],
            inc=1,
            device_id=(lax.rem(part + step, parts), me),
            device_id_type=MESH,
        )

    def exchange(source, target, index):
        @pl.loop(1, group)
        def _(step):
            peer = lax.rem(me + step, group)
            pltpu.make_async_remote_copy(
                src_ref=source.at[peer],
                dst_ref=target.at[me],
                send_sem=copy_sem.at[index, 0],
                recv_sem=copy_sem.at[index, 1],
                device_id=(part, peer),
                device_id_type=MESH,
            ).start()

    def arrived(buffer, index, count, side):
        some = buffer.at[pl.ds(0, count)]
        pltpu.make_async_copy(some, some, copy_sem.at[index, side]).wait()

    exchange(send_pair, recv_pair, 0)

    for step in range(1, parts):
        pl.semaphore_wait(ready_sem.at[step], 1)

    @pl.loop(0, half)
    def _(step):
        peer = half * (1 - core) + lax.rem(me + step, half)
        pltpu.make_async_remote_copy(
            src_ref=send_taps.at[peer],
            dst_ref=recv_taps.at[me],
            send_sem=copy_sem.at[1, 0],
            recv_sem=copy_sem.at[1, 1],
            device_id=(pair * 2 + my_half, peer),
            device_id_type=MESH,
        ).start()

    def to_core(source, target, index):
        copy = pltpu.make_async_remote_copy(
            src_ref=source,
            dst_ref=target,
            send_sem=core_sem.at[index, 0],
            recv_sem=core_sem.at[index, 1],
            device_id=(other, me),
            device_id_type=MESH,
        )
        copy.start()
        return copy

    for table in tables:
        table.wait()

    def twist(real_part, imag_part, slot):
        rows_here = pl.ds(slot * group, group)
        cosines, sines = twist_cos[...], twist_sin[...]
        turned[rows_here, pl.ds(0, rows)] = (real_part * cosines + imag_part * sines).astype(BF16)
        turned[rows_here, pl.ds(rows, rows)] = (imag_part * cosines - real_part * sines).astype(BF16)

    def stage_forward(buffer, slots, first):
        partial = dot(forward[...], buffer[...].reshape(2 * group, buffer.shape[2]))
        for offset, (r, j) in enumerate(slots):
            real_part = partial[2 * r * group : (2 * r + 1) * group, j * rows : (j + 1) * rows]
            imag_part = partial[(2 * r + 1) * group : (2 * r + 2) * group, j * rows : (j + 1) * rows]
            twist(real_part, imag_part, first + offset)
        here = pl.ds(first * group, len(slots) * group)
        spectrum[here, :] = dot(turned[here, :], inner_forward[...])

    def halves(slot):
        here = pl.ds(slot * group, group)
        return spectrum[here, pl.ds(0, rows)], spectrum[here, pl.ds(rows, rows)]

    def multiply(left, right, conjugate, slot):
        left_real, left_imag = halves(left)
        right_real, right_imag = halves(right)
        if conjugate:
            right_imag = -right_imag
        here = pl.ds(slot * group, group)
        product[here, pl.ds(0, rows)] = (left_real * right_real - left_imag * right_imag).astype(BF16)
        product[here, pl.ds(rows, rows)] = (left_real * right_imag + left_imag * right_real).astype(BF16)

    def stage_inverse(slots, first, target):
        here = pl.ds(first * group, len(slots) * group)
        back = dot(product[here, :], inner_inverse[...])
        cosines, sines = twist_cos[...], twist_sin[...]
        for offset, (r, j) in enumerate(slots):
            real_part = back[offset * group : (offset + 1) * group, :rows]
            imag_part = back[offset * group : (offset + 1) * group, rows:]
            across = pl.ds(j * rows, rows)
            untwisted[pl.ds(2 * r * group, group), across] = (real_part * cosines - imag_part * sines).astype(BF16)
            untwisted[pl.ds((2 * r + 1) * group, group), across] = (real_part * sines + imag_part * cosines).astype(BF16)
        width = target.shape[2]
        target[...] = dot(inverse[...], untwisted[:, pl.ds(0, width)]).astype(BF16).reshape(target.shape)

    pair_slots = [(r, j) for r in range(2) for j in range(lanes)]
    tap_slots = [(0, 0), (1, 0), (0, 1)]

    arrived(recv_taps, 1, half, 1)
    got = recv_taps.at[pl.ds(half * core, half)]
    taps_copy = to_core(got, got, 0)

    arrived(recv_pair, 0, group - 1, 1)
    stage_forward(recv_pair, pair_slots, 0)
    for i in range(lanes):
        multiply(lanes + i, i, True, i)
    untwisted[pl.ds(2 * group, 2 * group), pl.ds(rows, rows)] = jnp.zeros((2 * group, rows), BF16)
    stage_inverse(tap_slots, 0, send_filter)
    filter_copy = to_core(send_filter.at[pl.ds(half * core, half)], part_filter, 1)

    taps_copy.wait_recv()
    stage_forward(recv_taps, tap_slots, 2 * lanes)
    for i in range(lanes):
        multiply(i, 2 * lanes + i, False, i)
        multiply(lanes + i, 2 * lanes + i, True, lanes + i)
    stage_inverse(pair_slots, 0, send_back)
    exchange(send_back, recv_back, 2)
    recv_back[me] = send_back[me]

    filter_copy.wait_recv()
    kept = half * (1 - core)
    sum_filter[...] = (send_filter[pl.ds(kept, half)].astype(F32) + part_filter[...].astype(F32)).astype(BF16)
    for to_pair in range(parts // 2):

        @pl.loop(0, half)
        def _(step):
            peer = lax.rem(me + step, half)
            pltpu.make_async_remote_copy(
                src_ref=sum_filter.at[peer],
                dst_ref=recv_filter.at[pair, lax.rem(me, half)],
                send_sem=copy_sem.at[3, 0],
                recv_sem=copy_sem.at[3, 1],
                device_id=(to_pair * 2 + my_half, kept + peer),
                device_id_type=MESH,
            ).start()

    pltpu.make_async_copy(recv_filter, recv_filter, copy_sem.at[3, 1]).wait()
    total = recv_filter[0].astype(F32)
    for index in range(1, parts // 2):
        total = total + recv_filter[index].astype(F32)
    mine = all_filter.at[pl.ds(half * core, half)]
    mine[...] = total.astype(BF16)
    all_copy = to_core(mine, mine, 2)

    arrived(recv_back, 2, group - 1, 1)
    all_copy.wait_recv()
    arrived(send_pair, 0, group - 1, 0)
    arrived(send_taps, 1, half, 0)
    arrived(send_back, 2, group - 1, 0)
    pltpu.make_async_copy(recv_filter, recv_filter, copy_sem.at[3, 0]).wait()
    for copy in (taps_copy, filter_copy, all_copy):
        copy.wait_send()


def finish(
    group,
    queries,
    keys,
    values,
    cotangent,
    back,
    taps_back,
    pick,
    gated,
    grad_queries,
    grad_keys,
    grad_values,
    filter_grad,
):
    rows, channels = queries.shape
    lanes = channels // group
    spread = pick[...]
    flat = back[...].reshape(2 * group, lanes * rows)
    for i in range(lanes):
        both = dot(flat[:, i * rows : (i + 1) * rows], spread, (0, 0))
        conv, grad_mixed = both[:, :group], both[:, group:]
        here = pl.ds(i * group, group)
        gated[:, here] = (queries[:, here].astype(F32) * conv).astype(BF16)
        grad_queries[:, here] = (cotangent[:, here].astype(F32) * conv).astype(BF16)
        grad_keys[:, here] = (values[:, here].astype(F32) * grad_mixed).astype(BF16)
        grad_values[:, here] = (keys[:, here].astype(F32) * grad_mixed).astype(BF16)
    flat = taps_back[...].reshape(2 * group, 2 * rows)
    first = dot(flat[:, :rows], spread, (0, 0))
    filter_grad[:, pl.ds(0, 2 * group)] = first
    filter_grad[:, pl.ds(2 * group, group)] = dot(flat[:, rows:], spread, (0, 0))[:, :group]


def shards(group, parts, queries, keys, values, filter_taps, cotangent):
    rows, channels = filter_taps.shape
    lanes = channels // group
    tables = constant_tables(group, rows)
    vmem = pltpu.VMEM
    local = (rows, channels)
    pair = (group, 2, lanes * rows)
    single = (group, 2, 2 * rows)
    half = group // 2
    arrays = (queries[0], keys[0], values[0], filter_taps, cotangent[0])
    back, taps_back = pl.pallas_call(
        functools.partial(kernel, group, parts),
        out_shape=[jax.ShapeDtypeStruct(pair, BF16), jax.ShapeDtypeStruct(single, BF16)],
        in_specs=[pl.BlockSpec(memory_space=pl.ANY)] * 12,
        out_specs=[pl.BlockSpec(memory_space=vmem)] * 2,
        scratch_shapes=[vmem(local, BF16)] * 5
        + [vmem(table.shape, table.dtype) for table in tables]
        + [vmem(pair, BF16)] * 2
        + [vmem(single, BF16)] * 2
        + [vmem(pair, BF16)]
        + [vmem(single, BF16)]
        + [vmem((half,) + single[1:], BF16)] * 2
        + [
            vmem((parts // 2, half) + single[1:], BF16),
            vmem((3 * lanes * group, 2 * rows), BF16),
            vmem((3 * lanes * group, 2 * rows), F32),
            vmem((2 * lanes * group, 2 * rows), BF16),
            vmem((4 * group, lanes * rows), BF16),
            pltpu.SemaphoreType.DMA((6,)),
            pltpu.SemaphoreType.DMA((6,)),
            pltpu.SemaphoreType.DMA((4, 2)),
            pltpu.SemaphoreType.DMA((3, 2)),
            pltpu.SemaphoreType.REGULAR((parts,)),
        ],
        compiler_params=pltpu.CompilerParams(
            collective_id=0, has_side_effects=True, vmem_limit_bytes=60 << 20
        ),
    )(*arrays, *tables)
    outs = pl.pallas_call(
        functools.partial(finish, group),
        out_shape=[jax.ShapeDtypeStruct(local, BF16)] * 4 + [jax.ShapeDtypeStruct(local, F32)],
        in_specs=[pl.BlockSpec(memory_space=vmem)] * 7,
        out_specs=[pl.BlockSpec(memory_space=vmem)] * 5,
        compiler_params=pltpu.CompilerParams(vmem_limit_bytes=60 << 20),
    )(queries[0], keys[0], values[0], cotangent[0], back, taps_back, tables[4])
    return tuple(out[None] for out in outs[:4]) + (outs[4],)


def solution(mesh):
    spec = P("dp", "ctx", None)
    return jax.shard_map(
        functools.partial(shards, mesh.shape["ctx"], mesh.shape["dp"]),
        mesh=mesh,
        in_specs=(spec, spec, spec, P("ctx", None), spec),
        out_specs=(spec, spec, spec, spec, P("ctx", None)),
        check_vma=False,
    )
```

```python
import functools

import jax
import jax.numpy as jnp
import numpy as np
from jax import lax
from jax.experimental import pallas as pl
from jax.experimental.pallas import tpu as pltpu
from jax.sharding import PartitionSpec as P

MESH = pl.DeviceIdType.MESH
BF16 = jnp.bfloat16
F32 = jnp.float32


def dot(left, right, contract=(1, 0)):
    dims = (((contract[0],), (contract[1],)), ((), ()))
    return lax.dot_general(left, right, dims, preferred_element_type=F32)


def constant_tables(group, rows):
    total = group * rows
    outer = np.arange(group)
    inner = np.arange(rows)
    angle_outer = 2 * np.pi * np.outer(outer + 0.25, outer) / group
    angle_twist = 2 * np.pi * np.outer(outer + 0.25, inner) / total
    angle_inner = 2 * np.pi * np.outer(inner, inner) / rows
    cos_outer, sin_outer = np.cos(angle_outer), np.sin(angle_outer)
    forward = np.zeros((2, 2, group, group, 2))
    inverse = np.zeros((group, 2, 2, 2, group))
    scale = 1.0 / (total * np.sqrt(total))
    for slot in range(2):
        forward[slot, 0, :, :, slot] = cos_outer
        forward[slot, 1, :, :, slot] = -sin_outer
        inverse[:, slot, slot, 0, :] = cos_outer.T * scale
        inverse[:, slot, slot, 1, :] = -sin_outer.T * scale
    cos_inner, sin_inner = np.cos(angle_inner), np.sin(angle_inner)
    inner_forward = np.block([[cos_inner, -sin_inner], [sin_inner, cos_inner]])
    inner_inverse = np.block([[cos_inner, sin_inner], [-sin_inner, cos_inner]])
    pick = np.zeros((group, 2, 2, group))
    for slot in range(2):
        pick[outer, slot, slot, outer] = 1.0
    return (
        jnp.asarray(forward.reshape(4 * group, 2 * group), BF16),
        jnp.asarray(inverse.reshape(2 * group, 4 * group), BF16),
        jnp.asarray(inner_forward, BF16),
        jnp.asarray(inner_inverse, BF16),
        jnp.asarray(pick.reshape(2 * group, 2 * group), BF16),
        jnp.asarray(np.cos(angle_twist), F32),
        jnp.asarray(np.sin(angle_twist), F32),
    )


GRID = (8, 4, 4)


def far_first(count, step):
    return count // 2 + (step + 1) // 2 * (1 - 2 * (step % 2))


def planes(me):
    _, wide, deep = GRID
    x, z = lax.rem(me // deep, wide), lax.rem(me, deep)
    xs = [lax.rem(x + far_first(wide, step), wide) * deep for step in range(wide)]
    zs = [lax.rem(z + far_first(deep, step), deep) for step in range(deep)]
    return [one + two for one in xs for two in zs]


def others(me, act, steps, own_row):
    rows, wide, deep = GRID
    y = me // (wide * deep)
    plane = planes(me)

    @pl.loop(steps[0], steps[1])
    def _(step):
        offset = rows // 2 + (step + 1) // 2 * (1 - 2 * lax.rem(step, 2))
        act(lax.rem(y + offset, rows), plane)

    if own_row:
        act(y, plane[:-1])


def kernel(
    group,
    parts,
    queries,
    keys,
    values,
    taps,
    cotangent,
    forward_hbm,
    inverse_hbm,
    inner_forward_hbm,
    inner_inverse_hbm,
    pick_hbm,
    twist_cos_hbm,
    twist_sin_hbm,
    recv_back,
    q_buf,
    k_buf,
    v_buf,
    t_buf,
    c_buf,
    forward,
    inverse,
    inner_forward,
    inner_inverse,
    pick,
    twist_cos,
    twist_sin,
    send_there,
    recv_there,
    send_back,
    send_filter,
    part_filter,
    cross_filter,
    turned,
    spectrum,
    product,
    untwisted,
    in_sem,
    table_sem,
    copy_sem,
    core_sem,
    ready_sem,
):
    me = lax.axis_index("ctx")
    part = lax.axis_index("dp")
    core = lax.rem(part, 2)
    pair = part // 2
    twin = pair * 2 + 1 - core
    half = group // 2
    rows_all, wide, deep = GRID
    plane = wide * deep
    mine = lax.rem(me // half + core, 2)
    theirs = 1 - mine
    mate = lax.rem(pair + 1, parts // 2) * 2 + core
    lanes = queries.shape[1] // group
    rows = queries.shape[0]

    barrier = pltpu.get_barrier_semaphore()

    def greet(row, places):
        for place in places:
            pl.semaphore_signal(
                barrier, inc=1, device_id=(part, row * plane + place), device_id_type=MESH
            )

    pl.semaphore_signal(barrier, inc=1, device_id=(mate, me), device_id_type=MESH)
    others(me, greet, (0, rows_all - 1), True)
    pl.semaphore_signal(barrier, inc=1, device_id=(twin, me), device_id_type=MESH)

    loads = [
        pltpu.make_async_copy(source, target, in_sem.at[index])
        for index, (source, target) in enumerate(
            [(keys, k_buf), (values, v_buf), (queries, q_buf), (cotangent, c_buf), (taps, t_buf), (pick_hbm, pick)]
        )
    ]
    tables = [
        pltpu.make_async_copy(source, target, table_sem.at[index])
        for index, (source, target) in enumerate(
            [
                (forward_hbm, forward),
                (twist_cos_hbm, twist_cos),
                (twist_sin_hbm, twist_sin),
                (inner_forward_hbm, inner_forward),
                (inner_inverse_hbm, inner_inverse),
                (inverse_hbm, inverse),
            ]
        )
    ]
    for load in loads + tables:
        load.start()

    for load in loads:
        load.wait()

    def keep_own(source, target):
        here = pl.ds(0, lanes * rows)
        target[me, :, here] = source[me, :, here]

        @pl.when(core == 0)
        def _():
            here = pl.ds(lanes * rows, 2 * rows)
            target[me, :, here] = source[me, :, here]

    mixed = (k_buf[...].astype(F32) * v_buf[...].astype(F32)).astype(BF16)
    grad_conv = (c_buf[...].astype(F32) * q_buf[...].astype(F32)).astype(BF16)
    spread = pick[...]

    def block(array, index):
        return array[:, index * group : (index + 1) * group]

    pairs = jnp.concatenate(
        [jnp.concatenate([block(mixed, i), block(grad_conv, i)], axis=1) for i in range(lanes)], axis=0
    )
    width = lanes * rows
    there = dot(spread, pairs, (1, 1)).astype(BF16)
    send_there[:, :, pl.ds(0, width)] = there.reshape(group, 2, width)
    tap_rows = t_buf[...]
    tap_pairs = jnp.concatenate(
        [
            jnp.concatenate([block(tap_rows, 0), block(tap_rows, 1)], axis=1),
            jnp.concatenate([block(tap_rows, 2), jnp.zeros((rows, group), BF16)], axis=1),
        ],
        axis=0,
    )
    there = dot(spread, tap_pairs, (1, 1)).astype(BF16)
    send_there[:, :, pl.ds(width, 2 * rows)] = there.reshape(group, 2, 2 * rows)
    keep_own(send_there, recv_there)

    pl.semaphore_wait(barrier, group - 1 + 2)
    pl.semaphore_signal(ready_sem, inc=1, device_id=(mate, me), device_id_type=MESH)

    def remote(source, target, peer_part, peer, index):
        return pltpu.make_async_remote_copy(
            src_ref=source,
            dst_ref=target,
            send_sem=copy_sem.at[index, 0],
            recv_sem=copy_sem.at[index, 1],
            device_id=(peer_part, peer),
            device_id_type=MESH,
        )

    def exchange(source, target, index, steps, own_row):
        def send(row, places):
            whole = row // (rows_all // 2) == mine

            @pl.when(whole)
            def _():
                for place in places:
                    peer = row * plane + place
                    remote(source.at[peer], target.at[me], part, peer, index).start()

            @pl.when(jnp.logical_not(whole))
            def _():
                here = pl.ds(0, width)
                for place in places:
                    peer = row * plane + place
                    remote(source.at[peer, :, here], target.at[me, :, here], part, peer, index + 1).start()

        others(me, send, steps, own_row)

    def wait_bytes(some, sem):
        pltpu.make_async_copy(some, some, sem).wait()

    def finished(buffer, index, side):
        for value in range(2):

            @pl.when(core == value)
            def _():
                wait_bytes(buffer.at[pl.ds(0, half - 1 + value)], copy_sem.at[index, side])
                wait_bytes(buffer.at[pl.ds(0, half - value), :, pl.ds(0, width)], copy_sem.at[index + 1, side])

    first, rest = pl.ds(0, width), pl.ds(width, 2 * rows)

    def send_first(row, places):
        for place in places:
            peer = row * plane + place
            remote(send_there.at[peer, :, first], recv_there.at[me, :, first], part, peer, 0).start()

    def send_rest(row, places):
        @pl.when(row // (rows_all // 2) == mine)
        def _():
            for place in places:
                peer = row * plane + place
                remote(send_there.at[peer, :, rest], recv_there.at[me, :, rest], part, peer, 1).start()

    others(me, send_first, (0, rows_all - 1), True)
    others(me, send_rest, (0, rows_all - 1), True)

    def finished_first(side):
        wait_bytes(recv_there.at[pl.ds(0, group - 1), :, first], copy_sem.at[0, side])

    def finished_rest(side):
        for value in range(2):

            @pl.when(core == value)
            def _():
                wait_bytes(recv_there.at[pl.ds(0, half - 1 + value), :, rest], copy_sem.at[1, side])


    def to_core(source, target, index):
        return pltpu.make_async_remote_copy(
            src_ref=source,
            dst_ref=target,
            send_sem=core_sem.at[index, 0],
            recv_sem=core_sem.at[index, 1],
            device_id=(twin, me),
            device_id_type=MESH,
        )

    def second(buffer, which):
        return buffer.at[pl.ds(which * half, half), :, pl.ds(width, 2 * rows)]

    for table in tables:
        table.wait()

    def twist(real_part, imag_part, slot):
        rows_here = pl.ds(slot * group, group)
        cosines, sines = twist_cos[...], twist_sin[...]
        turned[rows_here, pl.ds(0, rows)] = (real_part * cosines + imag_part * sines).astype(BF16)
        turned[rows_here, pl.ds(rows, rows)] = (imag_part * cosines - real_part * sines).astype(BF16)

    def stage_forward(buffer, slots, first):
        partial = dot(forward[...], buffer.reshape(2 * group, buffer.shape[2]))
        for offset, (r, j) in enumerate(slots):
            real_part = partial[2 * r * group : (2 * r + 1) * group, j * rows : (j + 1) * rows]
            imag_part = partial[(2 * r + 1) * group : (2 * r + 2) * group, j * rows : (j + 1) * rows]
            twist(real_part, imag_part, first + offset)
        here = pl.ds(first * group, len(slots) * group)
        spectrum[here, :] = dot(turned[here, :], inner_forward[...])

    def halves(slot):
        here = pl.ds(slot * group, group)
        return spectrum[here, pl.ds(0, rows)], spectrum[here, pl.ds(rows, rows)]

    def multiply(left, right, conjugate, slot):
        left_real, left_imag = halves(left)
        right_real, right_imag = halves(right)
        if conjugate:
            right_imag = -right_imag
        here = pl.ds(slot * group, group)
        product[here, pl.ds(0, rows)] = (left_real * right_real - left_imag * right_imag).astype(BF16)
        product[here, pl.ds(rows, rows)] = (left_real * right_imag + left_imag * right_real).astype(BF16)

    def stage_inverse(slots, first, target):
        here = pl.ds(first * group, len(slots) * group)
        back = dot(product[here, :], inner_inverse[...])
        cosines, sines = twist_cos[...], twist_sin[...]
        for offset, (r, j) in enumerate(slots):
            real_part = back[offset * group : (offset + 1) * group, :rows]
            imag_part = back[offset * group : (offset + 1) * group, rows:]
            across = pl.ds(j * rows, rows)
            untwisted[pl.ds(2 * r * group, group), across] = (real_part * cosines - imag_part * sines).astype(BF16)
            untwisted[pl.ds((2 * r + 1) * group, group), across] = (real_part * sines + imag_part * cosines).astype(BF16)
        size = (slots[-1][1] + 1) * rows
        back = dot(inverse[...], untwisted[:, pl.ds(0, size)]).astype(BF16)
        target[:, :, pl.ds(0, size)] = back.reshape(group, 2, size)

    pair_slots = [(r, j) for r in range(2) for j in range(lanes)]
    tap_slots = [(0, 0), (1, 0), (0, 1)]

    finished_first(1)
    stage_forward(recv_there[:, :, first], pair_slots, 0)
    for i in range(lanes):
        multiply(lanes + i, i, True, i)
    untwisted[pl.ds(2 * group, 2 * group), pl.ds(rows, rows)] = jnp.zeros((2 * group, rows), BF16)
    stage_inverse(tap_slots, 0, send_filter)
    filter_copy = to_core(send_filter.at[pl.ds(theirs * half, half)], part_filter, 1)
    filter_copy.start()
    finished_rest(1)
    taps_copy = to_core(second(recv_there, mine), second(recv_there, mine), 0)
    taps_copy.start()

    filter_copy.wait_recv()
    both = send_filter[pl.ds(mine * half, half)].astype(F32) + part_filter[...].astype(F32)
    send_back[pl.ds(mine * half, half), :, rest] = both.astype(BF16)
    pl.semaphore_wait(ready_sem, 1)

    def cross(row, places):
        @pl.when(row // (rows_all // 2) == mine)
        def _():
            for place in places:
                peer = row * plane + place
                remote(
                    send_back.at[peer, :, rest], cross_filter.at[lax.rem(me, half)], mate, peer, 4
                ).start()

    others(me, cross, (0, rows_all), False)

    taps_copy.wait_recv()
    stage_forward(recv_there[:, :, rest], tap_slots, 2 * lanes)
    for i in range(lanes):
        multiply(i, 2 * lanes + i, False, i)
        multiply(lanes + i, 2 * lanes + i, True, lanes + i)
    stage_inverse(pair_slots, 0, send_back)
    keep_own(send_back, recv_back)
    exchange(send_back, recv_back, 2, (0, rows_all - 1), True)

    finished(recv_back, 2, 1)
    wait_bytes(cross_filter, copy_sem.at[4, 1])
    here = second(recv_back, mine)
    here[...] = (here[...].astype(F32) + cross_filter[...].astype(F32)).astype(BF16)
    all_copy = to_core(here, here, 2)
    all_copy.start()
    finished_first(0)
    finished_rest(0)
    finished(send_back, 2, 0)
    wait_bytes(cross_filter, copy_sem.at[4, 0])
    all_copy.wait_recv()
    for copy in (taps_copy, filter_copy, all_copy):
        copy.wait_send()


def finish(
    group,
    queries,
    keys,
    values,
    cotangent,
    back,
    pick,
    gated,
    grad_queries,
    grad_keys,
    grad_values,
    filter_grad,
):
    rows, channels = queries.shape
    lanes = channels // group
    spread = pick[...]
    width = back.shape[2]
    flat = back[...].reshape(2 * group, width)
    for i in range(lanes):
        both = dot(flat[:, i * rows : (i + 1) * rows], spread, (0, 0))
        conv, grad_mixed = both[:, :group], both[:, group:]
        here = pl.ds(i * group, group)
        gated[:, here] = (queries[:, here].astype(F32) * conv).astype(BF16)
        grad_queries[:, here] = (cotangent[:, here].astype(F32) * conv).astype(BF16)
        grad_keys[:, here] = (values[:, here].astype(F32) * grad_mixed).astype(BF16)
        grad_values[:, here] = (keys[:, here].astype(F32) * grad_mixed).astype(BF16)
    flat = flat[:, lanes * rows :]
    first = dot(flat[:, :rows], spread, (0, 0))
    filter_grad[:, pl.ds(0, 2 * group)] = first
    filter_grad[:, pl.ds(2 * group, group)] = dot(flat[:, rows:], spread, (0, 0))[:, :group]


def shards(group, parts, queries, keys, values, filter_taps, cotangent):
    rows, channels = filter_taps.shape
    lanes = channels // group
    tables = constant_tables(group, rows)
    vmem = pltpu.VMEM
    local = (rows, channels)
    block = (group, 2, (lanes + 2) * rows)
    single = (group, 2, 2 * rows)
    half = group // 2
    arrays = (queries[0], keys[0], values[0], filter_taps, cotangent[0])
    back = pl.pallas_call(
        functools.partial(kernel, group, parts),
        out_shape=jax.ShapeDtypeStruct(block, BF16),
        in_specs=[pl.BlockSpec(memory_space=pl.ANY)] * 12,
        out_specs=pl.BlockSpec(memory_space=vmem),
        scratch_shapes=[vmem(local, BF16)] * 5
        + [vmem(table.shape, table.dtype) for table in tables]
        + [vmem(block, BF16)] * 3
        + [vmem(single, BF16)]
        + [vmem((half,) + single[1:], BF16)] * 2
        + [
            vmem((3 * lanes * group, 2 * rows), BF16),
            vmem((3 * lanes * group, 2 * rows), F32),
            vmem((2 * lanes * group, 2 * rows), BF16),
            vmem((4 * group, lanes * rows), BF16),
            pltpu.SemaphoreType.DMA((6,)),
            pltpu.SemaphoreType.DMA((6,)),
            pltpu.SemaphoreType.DMA((5, 2)),
            pltpu.SemaphoreType.DMA((3, 2)),
            pltpu.SemaphoreType.REGULAR,
        ],
        compiler_params=pltpu.CompilerParams(
            collective_id=0, has_side_effects=True, vmem_limit_bytes=60 << 20
        ),
    )(*arrays, *tables)
    outs = pl.pallas_call(
        functools.partial(finish, group),
        out_shape=[jax.ShapeDtypeStruct(local, BF16)] * 4 + [jax.ShapeDtypeStruct(local, F32)],
        in_specs=[pl.BlockSpec(memory_space=vmem)] * 6,
        out_specs=[pl.BlockSpec(memory_space=vmem)] * 5,
        compiler_params=pltpu.CompilerParams(vmem_limit_bytes=60 << 20),
    )(queries[0], keys[0], values[0], cotangent[0], back, tables[4])
    return tuple(out[None] for out in outs[:4]) + (outs[4],)


def solution(mesh):
    spec = P("dp", "ctx", None)
    return jax.shard_map(
        functools.partial(shards, mesh.shape["ctx"], mesh.shape["dp"]),
        mesh=mesh,
        in_specs=(spec, spec, spec, P("ctx", None), spec),
        out_specs=(spec, spec, spec, spec, P("ctx", None)),
        check_vma=False,
    )
```

```python
import functools

import jax
import jax.numpy as jnp
import numpy as np
from jax import lax
from jax.experimental import pallas as pl
from jax.experimental.pallas import tpu as pltpu
from jax.sharding import PartitionSpec as P

MESH = pl.DeviceIdType.MESH
BF16 = jnp.bfloat16
F32 = jnp.float32


def dot(left, right, contract=(1, 0)):
    dims = (((contract[0],), (contract[1],)), ((), ()))
    return lax.dot_general(left, right, dims, preferred_element_type=F32)


def constant_tables(group, rows):
    total = group * rows
    outer = np.arange(group)
    inner = np.arange(rows)
    angle_outer = 2 * np.pi * np.outer(outer + 0.25, outer) / group
    angle_twist = 2 * np.pi * np.outer(outer + 0.25, inner) / total
    angle_inner = 2 * np.pi * np.outer(inner, inner) / rows
    cos_outer, sin_outer = np.cos(angle_outer), np.sin(angle_outer)
    forward = np.zeros((2, 2, group, group, 2))
    inverse = np.zeros((group, 2, 2, 2, group))
    scale = 1.0 / (total * np.sqrt(total))
    for slot in range(2):
        forward[slot, 0, :, :, slot] = cos_outer
        forward[slot, 1, :, :, slot] = -sin_outer
        inverse[:, slot, slot, 0, :] = cos_outer.T * scale
        inverse[:, slot, slot, 1, :] = -sin_outer.T * scale
    cos_inner, sin_inner = np.cos(angle_inner), np.sin(angle_inner)
    inner_forward = np.block([[cos_inner, -sin_inner], [sin_inner, cos_inner]])
    inner_inverse = np.block([[cos_inner, sin_inner], [-sin_inner, cos_inner]])
    pick = np.zeros((group, 2, 2, group))
    for slot in range(2):
        pick[outer, slot, slot, outer] = 1.0
    inverse = inverse.reshape(2 * group, 4 * group)
    squares = [
        forward.reshape(4 * group, 2 * group),
        inner_forward,
        inner_inverse,
        inverse[:, : 2 * group],
        inverse[:, 2 * group :],
        pick.reshape(2 * group, 2 * group),
    ]
    twists = np.stack([np.cos(angle_twist), np.sin(angle_twist)])
    return jnp.asarray(np.concatenate(squares), BF16), jnp.asarray(twists, F32)


KERNEL_VMEM = 54613 << 10

GRID = (8, 4, 4)


def far_first(count, step):
    return count // 2 + (step + 1) // 2 * (1 - 2 * (step % 2))


def planes(me):
    _, wide, deep = GRID
    x, z = lax.rem(me // deep, wide), lax.rem(me, deep)
    xs = [lax.rem(x + far_first(wide, step), wide) * deep for step in range(wide)]
    zs = [lax.rem(z + far_first(deep, step), deep) for step in range(deep)]
    return [one + two for one in xs for two in zs]


def others(me, act, steps, own_row):
    rows, wide, deep = GRID
    y = me // (wide * deep)
    plane = planes(me)

    @pl.loop(steps[0], steps[1])
    def _(step):
        offset = rows // 2 + (step + 1) // 2 * (1 - 2 * lax.rem(step, 2))
        act(lax.rem(y + offset, rows), plane)

    if own_row:
        act(y, plane[:-1])


def kernel(
    group,
    parts,
    queries,
    keys,
    values,
    taps,
    cotangent,
    tables_hbm,
    twists_hbm,
    gated,
    grad_queries,
    grad_keys,
    grad_values,
    filter_first,
    filter_second,
    filter_third,
    recv_back,
    q_buf,
    k_buf,
    v_buf,
    t_buf,
    c_buf,
    forward,
    inverse,
    inner_forward,
    inner_inverse,
    pick,
    twist_cos,
    twist_sin,
    send_there,
    recv_there,
    send_back,
    send_filter,
    part_filter,
    cross_filter,
    turned,
    spectrum,
    product,
    untwisted,
    in_sem,
    table_sem,
    copy_sem,
    core_sem,
    ready_sem,
):
    me = lax.axis_index("ctx")
    part = lax.axis_index("dp")
    core = lax.rem(part, 2)
    pair = part // 2
    twin = pair * 2 + 1 - core
    half = group // 2
    rows_all, wide, deep = GRID
    plane = wide * deep
    mine = lax.rem(me // half + core, 2)
    theirs = 1 - mine
    mate = lax.rem(pair + 1, parts // 2) * 2 + core
    lanes = queries.shape[1] // group
    rows = queries.shape[0]

    def table(index):
        return tables_hbm.at[pl.ds(index * 2 * group, 2 * group)]

    loads = [
        pltpu.make_async_copy(source, target, in_sem.at[index])
        for index, (source, target) in enumerate(
            [(keys, k_buf), (values, v_buf), (queries, q_buf), (cotangent, c_buf), (taps, t_buf), (table(6), pick)]
        )
    ]
    for load in loads:
        load.start()
    barrier = pltpu.get_barrier_semaphore()

    def greet(row, places):
        for place in places:
            pl.semaphore_signal(
                barrier, inc=1, device_id=(part, row * plane + place), device_id_type=MESH
            )

    pl.semaphore_signal(barrier, inc=1, device_id=(mate, me), device_id_type=MESH)
    others(me, greet, (0, rows_all - 1), True)
    pl.semaphore_signal(barrier, inc=1, device_id=(twin, me), device_id_type=MESH)

    tables = [
        pltpu.make_async_copy(source, target, table_sem.at[index])
        for index, (source, target) in enumerate(
            [
                (table(0), forward.at[pl.ds(0, 2 * group)]),
                (table(1), forward.at[pl.ds(2 * group, 2 * group)]),
                (twists_hbm.at[0], twist_cos),
                (twists_hbm.at[1], twist_sin),
                (table(2), inner_forward),
                (table(3), inner_inverse),
                (table(4), inverse.at[0]),
                (table(5), inverse.at[1]),
            ]
        )
    ]
    for load in tables:
        load.start()

    for load in loads:
        load.wait()

    def keep_own(source, target):
        here = pl.ds(0, lanes * rows)
        target[me, :, here] = source[me, :, here]

        @pl.when(core == 0)
        def _():
            here = pl.ds(lanes * rows, 2 * rows)
            target[me, :, here] = source[me, :, here]

    mixed = (k_buf[...].astype(F32) * v_buf[...].astype(F32)).astype(BF16)
    grad_conv = (c_buf[...].astype(F32) * q_buf[...].astype(F32)).astype(BF16)
    spread = pick[...]

    def block(array, index):
        return array[:, index * group : (index + 1) * group]

    pairs = jnp.concatenate(
        [jnp.concatenate([block(mixed, i), block(grad_conv, i)], axis=1) for i in range(lanes)], axis=0
    )
    width = lanes * rows
    there = dot(spread, pairs, (1, 1)).astype(BF16)
    send_there[:, :, pl.ds(0, width)] = there.reshape(group, 2, width)
    tap_rows = t_buf[...]
    tap_pairs = jnp.concatenate(
        [
            jnp.concatenate([block(tap_rows, 0), block(tap_rows, 1)], axis=1),
            jnp.concatenate([block(tap_rows, 2), jnp.zeros((rows, group), BF16)], axis=1),
        ],
        axis=0,
    )
    there = dot(spread, tap_pairs, (1, 1)).astype(BF16)
    send_there[:, :, pl.ds(width, 2 * rows)] = there.reshape(group, 2, 2 * rows)
    keep_own(send_there, recv_there)

    pl.semaphore_wait(barrier, group - 1 + 2)
    pl.semaphore_signal(ready_sem, inc=1, device_id=(mate, me), device_id_type=MESH)

    def remote(source, target, peer_part, peer, index):
        return pltpu.make_async_remote_copy(
            src_ref=source,
            dst_ref=target,
            send_sem=copy_sem.at[index, 0],
            recv_sem=copy_sem.at[index, 1],
            device_id=(peer_part, peer),
            device_id_type=MESH,
        )

    def exchange(source, target, index, steps, own_row):
        def send(row, places):
            whole = row // (rows_all // 2) == mine

            @pl.when(whole)
            def _():
                for place in places:
                    peer = row * plane + place
                    remote(source.at[peer], target.at[me], part, peer, index).start()

            @pl.when(jnp.logical_not(whole))
            def _():
                here = pl.ds(0, width)
                for place in places:
                    peer = row * plane + place
                    remote(source.at[peer, :, here], target.at[me, :, here], part, peer, index + 1).start()

        others(me, send, steps, own_row)

    def wait_bytes(some, sem):
        pltpu.make_async_copy(some, some, sem).wait()

    def finished(buffer, index, side):
        for value in range(2):

            @pl.when(core == value)
            def _():
                wait_bytes(buffer.at[pl.ds(0, half - 1 + value)], copy_sem.at[index, side])
                wait_bytes(buffer.at[pl.ds(0, half - value), :, pl.ds(0, width)], copy_sem.at[index + 1, side])

    first, rest = pl.ds(0, width), pl.ds(width, 2 * rows)

    def send_first(row, places):
        for place in places:
            peer = row * plane + place
            remote(send_there.at[peer, :, first], recv_there.at[me, :, first], part, peer, 0).start()

    def send_rest(row, places):
        @pl.when(row // (rows_all // 2) == mine)
        def _():
            for place in places:
                peer = row * plane + place
                remote(send_there.at[peer, :, rest], recv_there.at[me, :, rest], part, peer, 1).start()

    others(me, send_first, (0, rows_all - 1), True)
    others(me, send_rest, (0, rows_all - 1), True)

    def finished_first(side):
        wait_bytes(recv_there.at[pl.ds(0, group - 1), :, first], copy_sem.at[0, side])

    def finished_rest(side):
        for value in range(2):

            @pl.when(core == value)
            def _():
                wait_bytes(recv_there.at[pl.ds(0, half - 1 + value), :, rest], copy_sem.at[1, side])


    def to_core(source, target, index):
        return pltpu.make_async_remote_copy(
            src_ref=source,
            dst_ref=target,
            send_sem=core_sem.at[index, 0],
            recv_sem=core_sem.at[index, 1],
            device_id=(twin, me),
            device_id_type=MESH,
        )

    def second(buffer, which):
        return buffer.at[pl.ds(which * half, half), :, pl.ds(width, 2 * rows)]

    for load in tables:
        load.wait()

    def twist(real_part, imag_part, slot):
        rows_here = pl.ds(slot * group, group)
        cosines, sines = twist_cos[...], twist_sin[...]
        turned[rows_here, pl.ds(0, rows)] = (real_part * cosines + imag_part * sines).astype(BF16)
        turned[rows_here, pl.ds(rows, rows)] = (imag_part * cosines - real_part * sines).astype(BF16)

    def stage_forward(buffer, slots, first):
        partial = dot(forward[...], buffer.reshape(2 * group, buffer.shape[2]))
        for offset, (r, j) in enumerate(slots):
            real_part = partial[2 * r * group : (2 * r + 1) * group, j * rows : (j + 1) * rows]
            imag_part = partial[(2 * r + 1) * group : (2 * r + 2) * group, j * rows : (j + 1) * rows]
            twist(real_part, imag_part, first + offset)
        here = pl.ds(first * group, len(slots) * group)
        spectrum[here, :] = dot(turned[here, :], inner_forward[...])

    def halves(slot):
        here = pl.ds(slot * group, group)
        return spectrum[here, pl.ds(0, rows)], spectrum[here, pl.ds(rows, rows)]

    def multiply(left, right, conjugate, slot):
        left_real, left_imag = halves(left)
        right_real, right_imag = halves(right)
        if conjugate:
            right_imag = -right_imag
        here = pl.ds(slot * group, group)
        product[here, pl.ds(0, rows)] = (left_real * right_real - left_imag * right_imag).astype(BF16)
        product[here, pl.ds(rows, rows)] = (left_real * right_imag + left_imag * right_real).astype(BF16)

    def stage_inverse(slots, first, target):
        here = pl.ds(first * group, len(slots) * group)
        back = dot(product[here, :], inner_inverse[...])
        cosines, sines = twist_cos[...], twist_sin[...]
        for offset, (r, j) in enumerate(slots):
            real_part = back[offset * group : (offset + 1) * group, :rows]
            imag_part = back[offset * group : (offset + 1) * group, rows:]
            across = pl.ds(j * rows, rows)
            untwisted[pl.ds(2 * r * group, group), across] = (real_part * cosines - imag_part * sines).astype(BF16)
            untwisted[pl.ds((2 * r + 1) * group, group), across] = (real_part * sines + imag_part * cosines).astype(BF16)
        size = (slots[-1][1] + 1) * rows
        back = (
            dot(inverse[0], untwisted[pl.ds(0, 2 * group), pl.ds(0, size)])
            + dot(inverse[1], untwisted[pl.ds(2 * group, 2 * group), pl.ds(0, size)])
        ).astype(BF16)
        target[:, :, pl.ds(0, size)] = back.reshape(group, 2, size)

    pair_slots = [(r, j) for r in range(2) for j in range(lanes)]
    tap_slots = [(0, 0), (1, 0), (0, 1)]

    finished_first(1)
    stage_forward(recv_there[:, :, first], pair_slots, 0)
    for i in range(lanes):
        multiply(lanes + i, i, True, i)
    untwisted[pl.ds(2 * group, 2 * group), pl.ds(rows, rows)] = jnp.zeros((2 * group, rows), BF16)
    stage_inverse(tap_slots, 0, send_filter)
    filter_copy = to_core(send_filter.at[pl.ds(theirs * half, half)], part_filter, 1)
    filter_copy.start()
    finished_rest(1)
    taps_copy = to_core(second(recv_there, mine), second(recv_there, mine), 0)
    taps_copy.start()

    filter_copy.wait_recv()
    both = send_filter[pl.ds(mine * half, half)].astype(F32) + part_filter[...].astype(F32)
    send_back[pl.ds(mine * half, half), :, rest] = both.astype(BF16)
    pl.semaphore_wait(ready_sem, 1)

    def cross(row, places):
        @pl.when(row // (rows_all // 2) == mine)
        def _():
            for place in places:
                peer = row * plane + place
                remote(
                    send_back.at[peer, :, rest], cross_filter.at[lax.rem(me, half)], mate, peer, 4
                ).start()

    others(me, cross, (0, rows_all), False)

    taps_copy.wait_recv()
    stage_forward(recv_there[:, :, rest], tap_slots, 2 * lanes)
    for i in range(lanes):
        multiply(i, 2 * lanes + i, False, i)
        multiply(lanes + i, 2 * lanes + i, True, lanes + i)
    stage_inverse(pair_slots, 0, send_back)
    keep_own(send_back, recv_back)
    exchange(send_back, recv_back, 2, (0, rows_all - 1), True)

    finished(recv_back, 2, 1)
    wait_bytes(cross_filter, copy_sem.at[4, 1])
    here = second(recv_back, mine)
    here[...] = (here[...].astype(F32) + cross_filter[...].astype(F32)).astype(BF16)
    all_copy = to_core(here, here, 2)
    all_copy.start()
    flat = recv_back[:, :, first].reshape(2 * group, width)
    for i in range(lanes):
        both = dot(flat[:, i * rows : (i + 1) * rows], spread, (0, 0))
        conv, grad_mixed = both[:, :group], both[:, group:]
        here = pl.ds(i * group, group)
        gated[:, here] = (q_buf[:, here].astype(F32) * conv).astype(BF16)
        grad_queries[:, here] = (c_buf[:, here].astype(F32) * conv).astype(BF16)
        grad_keys[:, here] = (v_buf[:, here].astype(F32) * grad_mixed).astype(BF16)
        grad_values[:, here] = (k_buf[:, here].astype(F32) * grad_mixed).astype(BF16)
    all_copy.wait_recv()
    flat = recv_back[:, :, rest].reshape(2 * group, 2 * rows)
    both = dot(flat[:, :rows], spread, (0, 0))
    filter_first[...] = both[:, :group]
    filter_second[...] = both[:, group:]
    filter_third[...] = dot(flat[:, rows:], spread, (0, 0))[:, :group]
    finished_first(0)
    finished_rest(0)
    finished(send_back, 2, 0)
    wait_bytes(cross_filter, copy_sem.at[4, 0])
    for copy in (taps_copy, filter_copy, all_copy):
        copy.wait_send()


def hand_over(gated, grad_queries, grad_keys, grad_values, first, second, third, *refs):
    *targets, filter_grad, sems = refs
    group = first.shape[1]
    pairs = list(zip((gated, grad_queries, grad_keys, grad_values), targets))
    for index, source in enumerate((first, second, third)):
        pairs.append((source, filter_grad.at[:, pl.ds(index * group, group)]))
    copies = [
        pltpu.make_async_copy(source, target, sems.at[index]) for index, (source, target) in enumerate(pairs)
    ]
    for copy in copies:
        copy.start()
    for copy in copies:
        copy.wait()


def shards(group, parts, queries, keys, values, filter_taps, cotangent):
    rows, channels = filter_taps.shape
    lanes = channels // group
    tables = constant_tables(group, rows)
    vmem = pltpu.VMEM
    local = (rows, channels)
    block = (group, 2, (lanes + 2) * rows)
    single = (group, 2, 2 * rows)
    half = group // 2
    arrays = (queries[0], keys[0], values[0], filter_taps, cotangent[0])
    results = [jax.ShapeDtypeStruct(local, BF16)] * 4 + [jax.ShapeDtypeStruct(local, F32)]
    outs = pl.pallas_call(
        functools.partial(kernel, group, parts),
        out_shape=results[:4] + [jax.ShapeDtypeStruct((rows, group), F32)] * lanes,
        in_specs=[pl.BlockSpec(memory_space=pl.ANY)] * 7,
        out_specs=[pl.BlockSpec(memory_space=vmem)] * (4 + lanes),
        scratch_shapes=[vmem(block, BF16)]
        + [vmem(local, BF16)] * 5
        + [vmem((4 * group, 2 * group), BF16), vmem((2, 2 * group, 2 * group), BF16)]
        + [vmem((2 * group, 2 * group), BF16)] * 3
        + [vmem((group, rows), F32)] * 2
        + [vmem(block, BF16)] * 3
        + [vmem(single, BF16)]
        + [vmem((half,) + single[1:], BF16)] * 2
        + [
            vmem((3 * lanes * group, 2 * rows), BF16),
            vmem((3 * lanes * group, 2 * rows), F32),
            vmem((2 * lanes * group, 2 * rows), BF16),
            vmem((4 * group, lanes * rows), BF16),
            pltpu.SemaphoreType.DMA((6,)),
            pltpu.SemaphoreType.DMA((8,)),
            pltpu.SemaphoreType.DMA((5, 2)),
            pltpu.SemaphoreType.DMA((3, 2)),
            pltpu.SemaphoreType.REGULAR,
        ],
        compiler_params=pltpu.CompilerParams(
            collective_id=0, has_side_effects=True, vmem_limit_bytes=KERNEL_VMEM
        ),
    )(*arrays, *tables)
    outs = pl.pallas_call(
        hand_over,
        out_shape=results,
        in_specs=[pl.BlockSpec(memory_space=vmem)] * (4 + lanes),
        out_specs=[pl.BlockSpec(memory_space=pl.ANY)] * 5,
        scratch_shapes=[pltpu.SemaphoreType.DMA((4 + lanes,))],
        compiler_params=pltpu.CompilerParams(vmem_limit_bytes=16 << 20),
    )(*outs)
    return tuple(out[None] for out in outs[:4]) + (outs[4],)


def solution(mesh):
    spec = P("dp", "ctx", None)
    return jax.shard_map(
        functools.partial(shards, mesh.shape["ctx"], mesh.shape["dp"]),
        mesh=mesh,
        in_specs=(spec, spec, spec, P("ctx", None), spec),
        out_specs=(spec, spec, spec, spec, P("ctx", None)),
        check_vma=False,
    )
```

```python
import functools

import jax
import jax.numpy as jnp
import numpy as np
from jax import lax
from jax.experimental import pallas as pl
from jax.experimental.pallas import tpu as pltpu
from jax.sharding import PartitionSpec as P

MESH = pl.DeviceIdType.MESH
BF16 = jnp.bfloat16
F32 = jnp.float32


def dot(left, right, contract=(1, 0)):
    dims = (((contract[0],), (contract[1],)), ((), ()))
    return lax.dot_general(left, right, dims, preferred_element_type=F32)


def constant_tables(group, rows):
    total = group * rows
    outer = np.arange(group)
    inner = np.arange(rows)
    angle_outer = 2 * np.pi * np.outer(outer + 0.25, outer) / group
    angle_twist = 2 * np.pi * np.outer(outer + 0.25, inner) / total
    angle_inner = 2 * np.pi * np.outer(inner, inner) / rows
    cos_outer, sin_outer = np.cos(angle_outer), np.sin(angle_outer)
    forward = np.zeros((2, 2, group, group, 2))
    inverse = np.zeros((group, 2, 2, 2, group))
    scale = 1.0 / (total * np.sqrt(total))
    for slot in range(2):
        forward[slot, 0, :, :, slot] = cos_outer
        forward[slot, 1, :, :, slot] = -sin_outer
        inverse[:, slot, slot, 0, :] = cos_outer.T * scale
        inverse[:, slot, slot, 1, :] = -sin_outer.T * scale
    cos_inner, sin_inner = np.cos(angle_inner), np.sin(angle_inner)
    inner_forward = np.block([[cos_inner, -sin_inner], [sin_inner, cos_inner]])
    inner_inverse = np.block([[cos_inner, sin_inner], [-sin_inner, cos_inner]])
    pick = np.zeros((group, 2, 2, group))
    for slot in range(2):
        pick[outer, slot, slot, outer] = 1.0
    inverse = inverse.reshape(2 * group, 4 * group)
    squares = [
        forward.reshape(4 * group, 2 * group),
        inner_forward,
        inner_inverse,
        inverse[:, : 2 * group],
        inverse[:, 2 * group :],
        pick.reshape(2 * group, 2 * group),
    ]
    twists = np.stack([np.cos(angle_twist), np.sin(angle_twist)])
    return jnp.asarray(np.concatenate(squares), BF16), jnp.asarray(twists, F32)


KERNEL_VMEM = 54613 << 10

GRID = (8, 4, 4)


def far_first(count, step):
    return count // 2 + (step + 1) // 2 * (1 - 2 * (step % 2))


def planes(me):
    _, wide, deep = GRID
    x, z = lax.rem(me // deep, wide), lax.rem(me, deep)
    xs = [lax.rem(x + far_first(wide, step), wide) * deep for step in range(wide)]
    zs = [lax.rem(z + far_first(deep, step), deep) for step in range(deep)]
    return [one + two for one in xs for two in zs]


def others(me, act, steps, own_row):
    rows, wide, deep = GRID
    y = me // (wide * deep)
    plane = planes(me)

    @pl.loop(steps[0], steps[1])
    def _(step):
        offset = rows // 2 + (step + 1) // 2 * (1 - 2 * lax.rem(step, 2))
        act(lax.rem(y + offset, rows), plane)

    if own_row:
        act(y, plane[:-1])


def kernel(
    group,
    parts,
    queries,
    keys,
    values,
    taps,
    cotangent,
    tables_hbm,
    twists_hbm,
    gated,
    grad_queries,
    grad_keys,
    grad_values,
    filter_first,
    filter_second,
    filter_third,
    recv_back,
    q_buf,
    k_buf,
    v_buf,
    t_buf,
    c_buf,
    forward,
    inverse,
    inner_forward,
    inner_inverse,
    pick,
    twist_cos,
    twist_sin,
    send_there,
    recv_there,
    send_back,
    send_filter,
    part_filter,
    cross_filter,
    turned,
    spectrum,
    product,
    untwisted,
    in_sem,
    table_sem,
    copy_sem,
    core_sem,
    ready_sem,
):
    me = lax.axis_index("ctx")
    part = lax.axis_index("dp")
    core = lax.rem(part, 2)
    pair = part // 2
    twin = pair * 2 + 1 - core
    half = group // 2
    rows_all, wide, deep = GRID
    plane = wide * deep
    mine = lax.rem(me // half + core, 2)
    theirs = 1 - mine
    mate = lax.rem(pair + 1, parts // 2) * 2 + core
    lanes = queries.shape[1] // group
    rows = queries.shape[0]

    def table(index):
        return tables_hbm.at[pl.ds(index * 2 * group, 2 * group)]

    loads = [
        pltpu.make_async_copy(source, target, in_sem.at[index])
        for index, (source, target) in enumerate(
            [(keys, k_buf), (values, v_buf), (queries, q_buf), (cotangent, c_buf), (taps, t_buf), (table(6), pick)]
        )
    ]
    for load in loads:
        load.start()
    barrier = pltpu.get_barrier_semaphore()

    def greet(row, places):
        for place in places:
            pl.semaphore_signal(
                barrier, inc=1, device_id=(part, row * plane + place), device_id_type=MESH
            )

    pl.semaphore_signal(barrier, inc=1, device_id=(mate, me), device_id_type=MESH)
    others(me, greet, (0, rows_all - 1), True)
    pl.semaphore_signal(barrier, inc=1, device_id=(twin, me), device_id_type=MESH)

    tables = [
        pltpu.make_async_copy(source, target, table_sem.at[index])
        for index, (source, target) in enumerate(
            [
                (table(0), forward.at[pl.ds(0, 2 * group)]),
                (table(1), forward.at[pl.ds(2 * group, 2 * group)]),
                (twists_hbm.at[0], twist_cos),
                (twists_hbm.at[1], twist_sin),
                (table(2), inner_forward),
                (table(3), inner_inverse),
                (table(4), inverse.at[0]),
                (table(5), inverse.at[1]),
            ]
        )
    ]
    for load in tables:
        load.start()

    for load in loads:
        load.wait()

    def keep_own(source, target):
        here = pl.ds(0, lanes * rows)
        target[me, :, here] = source[me, :, here]

        @pl.when(core == 0)
        def _():
            here = pl.ds(lanes * rows, 2 * rows)
            target[me, :, here] = source[me, :, here]

    mixed = (k_buf[...].astype(F32) * v_buf[...].astype(F32)).astype(BF16)
    grad_conv = (c_buf[...].astype(F32) * q_buf[...].astype(F32)).astype(BF16)
    spread = pick[...]

    def block(array, index):
        return array[:, index * group : (index + 1) * group]

    pairs = jnp.concatenate(
        [jnp.concatenate([block(mixed, i), block(grad_conv, i)], axis=1) for i in range(lanes)], axis=0
    )
    width = lanes * rows
    there = dot(spread, pairs, (1, 1)).astype(BF16)
    send_there[:, :, pl.ds(0, width)] = there.reshape(group, 2, width)
    tap_rows = t_buf[...]
    tap_pairs = jnp.concatenate(
        [
            jnp.concatenate([block(tap_rows, 0), block(tap_rows, 1)], axis=1),
            jnp.concatenate([block(tap_rows, 2), jnp.zeros((rows, group), BF16)], axis=1),
        ],
        axis=0,
    )
    there = dot(spread, tap_pairs, (1, 1)).astype(BF16)
    send_there[:, :, pl.ds(width, 2 * rows)] = there.reshape(group, 2, 2 * rows)
    keep_own(send_there, recv_there)

    pl.semaphore_wait(barrier, group - 1 + 2)
    pl.semaphore_signal(ready_sem, inc=1, device_id=(mate, me), device_id_type=MESH)

    def remote(source, target, peer_part, peer, index):
        return pltpu.make_async_remote_copy(
            src_ref=source,
            dst_ref=target,
            send_sem=copy_sem.at[index, 0],
            recv_sem=copy_sem.at[index, 1],
            device_id=(peer_part, peer),
            device_id_type=MESH,
        )

    def exchange(source, target, index, steps, own_row):
        def send(row, places):
            whole = row // (rows_all // 2) == mine

            @pl.when(whole)
            def _():
                for place in places:
                    peer = row * plane + place
                    remote(source.at[peer], target.at[me], part, peer, index).start()

            @pl.when(jnp.logical_not(whole))
            def _():
                here = pl.ds(0, width)
                for place in places:
                    peer = row * plane + place
                    remote(source.at[peer, :, here], target.at[me, :, here], part, peer, index + 1).start()

        others(me, send, steps, own_row)

    def wait_bytes(some, sem):
        pltpu.make_async_copy(some, some, sem).wait()

    def finished_whole(buffer, index, side):
        for value in range(2):

            @pl.when(core == value)
            def _():
                wait_bytes(buffer.at[pl.ds(0, half - 1 + value)], copy_sem.at[index, side])

    def finished_parts(buffer, index, side):
        for value in range(2):

            @pl.when(core == value)
            def _():
                wait_bytes(buffer.at[pl.ds(0, half - value), :, pl.ds(0, width)], copy_sem.at[index + 1, side])

    first, rest = pl.ds(0, width), pl.ds(width, 2 * rows)

    def send_first(row, places):
        for place in places:
            peer = row * plane + place
            remote(send_there.at[peer, :, first], recv_there.at[me, :, first], part, peer, 0).start()

    def send_rest(row, places):
        @pl.when(row // (rows_all // 2) == mine)
        def _():
            for place in places:
                peer = row * plane + place
                remote(send_there.at[peer, :, rest], recv_there.at[me, :, rest], part, peer, 1).start()

    others(me, send_first, (0, rows_all - 1), True)
    others(me, send_rest, (0, rows_all - 1), True)

    def finished_first(side):
        wait_bytes(recv_there.at[pl.ds(0, group - 1), :, first], copy_sem.at[0, side])

    def finished_rest(side):
        for value in range(2):

            @pl.when(core == value)
            def _():
                wait_bytes(recv_there.at[pl.ds(0, half - 1 + value), :, rest], copy_sem.at[1, side])


    def to_core(source, target, index):
        return pltpu.make_async_remote_copy(
            src_ref=source,
            dst_ref=target,
            send_sem=core_sem.at[index, 0],
            recv_sem=core_sem.at[index, 1],
            device_id=(twin, me),
            device_id_type=MESH,
        )

    def second(buffer, which):
        return buffer.at[pl.ds(which * half, half), :, pl.ds(width, 2 * rows)]

    for load in tables:
        load.wait()

    def twist(real_part, imag_part, slot):
        rows_here = pl.ds(slot * group, group)
        cosines, sines = twist_cos[...], twist_sin[...]
        turned[rows_here, pl.ds(0, rows)] = (real_part * cosines + imag_part * sines).astype(BF16)
        turned[rows_here, pl.ds(rows, rows)] = (imag_part * cosines - real_part * sines).astype(BF16)

    def stage_forward(buffer, slots, first):
        partial = dot(forward[...], buffer.reshape(2 * group, buffer.shape[2]))
        for offset, (r, j) in enumerate(slots):
            real_part = partial[2 * r * group : (2 * r + 1) * group, j * rows : (j + 1) * rows]
            imag_part = partial[(2 * r + 1) * group : (2 * r + 2) * group, j * rows : (j + 1) * rows]
            twist(real_part, imag_part, first + offset)
        here = pl.ds(first * group, len(slots) * group)
        spectrum[here, :] = dot(turned[here, :], inner_forward[...])

    def halves(slot):
        here = pl.ds(slot * group, group)
        return spectrum[here, pl.ds(0, rows)], spectrum[here, pl.ds(rows, rows)]

    def multiply(left, right, conjugate, slot):
        left_real, left_imag = halves(left)
        right_real, right_imag = halves(right)
        if conjugate:
            right_imag = -right_imag
        here = pl.ds(slot * group, group)
        product[here, pl.ds(0, rows)] = (left_real * right_real - left_imag * right_imag).astype(BF16)
        product[here, pl.ds(rows, rows)] = (left_real * right_imag + left_imag * right_real).astype(BF16)

    def stage_inverse(slots, first, target):
        here = pl.ds(first * group, len(slots) * group)
        back = dot(product[here, :], inner_inverse[...])
        cosines, sines = twist_cos[...], twist_sin[...]
        for offset, (r, j) in enumerate(slots):
            real_part = back[offset * group : (offset + 1) * group, :rows]
            imag_part = back[offset * group : (offset + 1) * group, rows:]
            across = pl.ds(j * rows, rows)
            untwisted[pl.ds(2 * r * group, group), across] = (real_part * cosines - imag_part * sines).astype(BF16)
            untwisted[pl.ds((2 * r + 1) * group, group), across] = (real_part * sines + imag_part * cosines).astype(BF16)
        size = (slots[-1][1] + 1) * rows
        back = (
            dot(inverse[0], untwisted[pl.ds(0, 2 * group), pl.ds(0, size)])
            + dot(inverse[1], untwisted[pl.ds(2 * group, 2 * group), pl.ds(0, size)])
        ).astype(BF16)
        target[:, :, pl.ds(0, size)] = back.reshape(group, 2, size)

    pair_slots = [(r, j) for r in range(2) for j in range(lanes)]
    tap_slots = [(0, 0), (1, 0), (0, 1)]

    finished_first(1)
    stage_forward(recv_there[:, :, first], pair_slots, 0)
    for i in range(lanes):
        multiply(lanes + i, i, True, i)
    untwisted[pl.ds(2 * group, 2 * group), pl.ds(rows, rows)] = jnp.zeros((2 * group, rows), BF16)
    stage_inverse(tap_slots, 0, send_filter)
    filter_copy = to_core(send_filter.at[pl.ds(theirs * half, half)], part_filter, 1)
    filter_copy.start()
    finished_rest(1)
    taps_copy = to_core(second(recv_there, mine), second(recv_there, mine), 0)
    taps_copy.start()

    filter_copy.wait_recv()
    both = send_filter[pl.ds(mine * half, half)].astype(F32) + part_filter[...].astype(F32)
    send_back[pl.ds(mine * half, half), :, rest] = both.astype(BF16)
    pl.semaphore_wait(ready_sem, 1)

    lines = rows_all // 2
    line = lax.rem(me // plane, lines)
    for step in range(lines):
        row = mine * lines + lax.rem(line + step, lines)
        for place in planes(me):
            peer = row * plane + place
            remote(send_back.at[peer, :, rest], cross_filter.at[lax.rem(me, half)], mate, peer, 4).start()

    taps_copy.wait_recv()
    stage_forward(recv_there[:, :, rest], tap_slots, 2 * lanes)
    for i in range(lanes):
        multiply(i, 2 * lanes + i, False, i)
        multiply(lanes + i, 2 * lanes + i, True, lanes + i)
    stage_inverse(pair_slots, 0, send_back)
    keep_own(send_back, recv_back)
    exchange(send_back, recv_back, 2, (0, rows_all - 1), True)

    finished_whole(recv_back, 2, 1)
    wait_bytes(cross_filter, copy_sem.at[4, 1])
    here = second(recv_back, mine)
    here[...] = (here[...].astype(F32) + cross_filter[...].astype(F32)).astype(BF16)
    all_copy = to_core(here, here, 2)
    all_copy.start()
    finished_parts(recv_back, 2, 1)
    flat = recv_back[:, :, first].reshape(2 * group, width)
    for i in range(lanes):
        both = dot(flat[:, i * rows : (i + 1) * rows], spread, (0, 0))
        conv, grad_mixed = both[:, :group], both[:, group:]
        here = pl.ds(i * group, group)
        gated[:, here] = (q_buf[:, here].astype(F32) * conv).astype(BF16)
        grad_queries[:, here] = (c_buf[:, here].astype(F32) * conv).astype(BF16)
        grad_keys[:, here] = (v_buf[:, here].astype(F32) * grad_mixed).astype(BF16)
        grad_values[:, here] = (k_buf[:, here].astype(F32) * grad_mixed).astype(BF16)
    all_copy.wait_recv()
    flat = recv_back[:, :, rest].reshape(2 * group, 2 * rows)
    both = dot(flat[:, :rows], spread, (0, 0))
    filter_first[...] = both[:, :group]
    filter_second[...] = both[:, group:]
    filter_third[...] = dot(flat[:, rows:], spread, (0, 0))[:, :group]
    finished_first(0)
    finished_rest(0)
    finished_whole(send_back, 2, 0)
    finished_parts(send_back, 2, 0)
    wait_bytes(cross_filter, copy_sem.at[4, 0])
    for copy in (taps_copy, filter_copy, all_copy):
        copy.wait_send()


def hand_over(gated, grad_queries, grad_keys, grad_values, first, second, third, *refs):
    *targets, filter_grad, sems = refs
    group = first.shape[1]
    pairs = list(zip((gated, grad_queries, grad_keys, grad_values), targets))
    for index, source in enumerate((first, second, third)):
        pairs.append((source, filter_grad.at[:, pl.ds(index * group, group)]))
    copies = [
        pltpu.make_async_copy(source, target, sems.at[index]) for index, (source, target) in enumerate(pairs)
    ]
    for copy in copies:
        copy.start()
    for copy in copies:
        copy.wait()


def shards(group, parts, queries, keys, values, filter_taps, cotangent):
    rows, channels = filter_taps.shape
    lanes = channels // group
    tables = constant_tables(group, rows)
    vmem = pltpu.VMEM
    local = (rows, channels)
    block = (group, 2, (lanes + 2) * rows)
    single = (group, 2, 2 * rows)
    half = group // 2
    arrays = (queries[0], keys[0], values[0], filter_taps, cotangent[0])
    results = [jax.ShapeDtypeStruct(local, BF16)] * 4 + [jax.ShapeDtypeStruct(local, F32)]
    outs = pl.pallas_call(
        functools.partial(kernel, group, parts),
        out_shape=results[:4] + [jax.ShapeDtypeStruct((rows, group), F32)] * lanes,
        in_specs=[pl.BlockSpec(memory_space=pl.ANY)] * 7,
        out_specs=[pl.BlockSpec(memory_space=vmem)] * (4 + lanes),
        scratch_shapes=[vmem(block, BF16)]
        + [vmem(local, BF16)] * 5
        + [vmem((4 * group, 2 * group), BF16), vmem((2, 2 * group, 2 * group), BF16)]
        + [vmem((2 * group, 2 * group), BF16)] * 3
        + [vmem((group, rows), F32)] * 2
        + [vmem(block, BF16)] * 3
        + [vmem(single, BF16)]
        + [vmem((half,) + single[1:], BF16)] * 2
        + [
            vmem((3 * lanes * group, 2 * rows), BF16),
            vmem((3 * lanes * group, 2 * rows), F32),
            vmem((2 * lanes * group, 2 * rows), BF16),
            vmem((4 * group, lanes * rows), BF16),
            pltpu.SemaphoreType.DMA((6,)),
            pltpu.SemaphoreType.DMA((8,)),
            pltpu.SemaphoreType.DMA((5, 2)),
            pltpu.SemaphoreType.DMA((3, 2)),
            pltpu.SemaphoreType.REGULAR,
        ],
        compiler_params=pltpu.CompilerParams(
            collective_id=0, has_side_effects=True, vmem_limit_bytes=KERNEL_VMEM
        ),
    )(*arrays, *tables)
    outs = pl.pallas_call(
        hand_over,
        out_shape=results,
        in_specs=[pl.BlockSpec(memory_space=vmem)] * (4 + lanes),
        out_specs=[pl.BlockSpec(memory_space=pl.ANY)] * 5,
        scratch_shapes=[pltpu.SemaphoreType.DMA((4 + lanes,))],
        compiler_params=pltpu.CompilerParams(vmem_limit_bytes=16 << 20),
    )(*outs)
    return tuple(out[None] for out in outs[:4]) + (outs[4],)


def solution(mesh):
    spec = P("dp", "ctx", None)
    return jax.shard_map(
        functools.partial(shards, mesh.shape["ctx"], mesh.shape["dp"]),
        mesh=mesh,
        in_specs=(spec, spec, spec, P("ctx", None), spec),
        out_specs=(spec, spec, spec, spec, P("ctx", None)),
        check_vma=False,
    )
```

```python
import functools

import jax
import jax.numpy as jnp
import numpy as np
from jax import lax
from jax.experimental import pallas as pl
from jax.experimental.pallas import tpu as pltpu
from jax.sharding import PartitionSpec as P

MESH = pl.DeviceIdType.MESH
BF16 = jnp.bfloat16
F32 = jnp.float32


def dot(left, right, contract=(1, 0)):
    dims = (((contract[0],), (contract[1],)), ((), ()))
    return lax.dot_general(left, right, dims, preferred_element_type=F32)


def constant_tables(group, rows):
    total = group * rows
    outer = np.arange(group)
    inner = np.arange(rows)
    angle_outer = 2 * np.pi * np.outer(outer + 0.25, outer) / group
    angle_twist = 2 * np.pi * np.outer(outer + 0.25, inner) / total
    angle_inner = 2 * np.pi * np.outer(inner, inner) / rows
    cos_outer, sin_outer = np.cos(angle_outer), np.sin(angle_outer)
    forward = np.zeros((2, 2, group, group, 2))
    inverse = np.zeros((group, 2, 2, 2, group))
    scale = 1.0 / (total * np.sqrt(total))
    for slot in range(2):
        forward[slot, 0, :, :, slot] = cos_outer
        forward[slot, 1, :, :, slot] = -sin_outer
        inverse[:, slot, slot, 0, :] = cos_outer.T * scale
        inverse[:, slot, slot, 1, :] = -sin_outer.T * scale
    cos_inner, sin_inner = np.cos(angle_inner), np.sin(angle_inner)
    inner_forward = np.block([[cos_inner, -sin_inner], [sin_inner, cos_inner]])
    inner_inverse = np.block([[cos_inner, sin_inner], [-sin_inner, cos_inner]])
    pick = np.zeros((group, 2, 2, group))
    for slot in range(2):
        pick[outer, slot, slot, outer] = 1.0
    inverse = inverse.reshape(2 * group, 4 * group)
    squares = [
        forward.reshape(4 * group, 2 * group),
        inner_forward,
        inner_inverse,
        inverse[:, : 2 * group],
        inverse[:, 2 * group :],
        pick.reshape(2 * group, 2 * group),
    ]
    twists = np.stack([np.cos(angle_twist), np.sin(angle_twist)])
    return jnp.asarray(np.concatenate(squares), BF16), jnp.asarray(twists, F32)


KERNEL_VMEM = 54613 << 10

GRID = (8, 4, 4)


def far_first(count, step):
    return count // 2 + (step + 1) // 2 * (1 - 2 * (step % 2))


def planes(me):
    _, wide, deep = GRID
    x, z = lax.rem(me // deep, wide), lax.rem(me, deep)
    xs = [lax.rem(x + far_first(wide, step), wide) * deep for step in range(wide)]
    zs = [lax.rem(z + far_first(deep, step), deep) for step in range(deep)]
    return [one + two for one in xs for two in zs]


def others(me, act, steps, own_row):
    rows, wide, deep = GRID
    y = me // (wide * deep)
    plane = planes(me)

    @pl.loop(steps[0], steps[1])
    def _(step):
        offset = rows // 2 + (step + 1) // 2 * (1 - 2 * lax.rem(step, 2))
        act(lax.rem(y + offset, rows), plane)

    if own_row:
        act(y, plane[:-1])


def kernel(
    group,
    parts,
    queries,
    keys,
    values,
    taps,
    cotangent,
    tables_hbm,
    twists_hbm,
    gated,
    grad_queries,
    grad_keys,
    grad_values,
    filter_first,
    filter_second,
    filter_third,
    recv_back,
    q_buf,
    k_buf,
    v_buf,
    t_buf,
    c_buf,
    forward,
    inverse,
    inner_forward,
    inner_inverse,
    pick,
    twist_cos,
    twist_sin,
    send_there,
    recv_there,
    send_back,
    send_filter,
    part_filter,
    cross_filter,
    turned,
    spectrum,
    product,
    untwisted,
    in_sem,
    table_sem,
    copy_sem,
    core_sem,
    ready_sem,
):
    me = lax.axis_index("ctx")
    part = lax.axis_index("dp")
    core = lax.rem(part, 2)
    pair = part // 2
    twin = pair * 2 + 1 - core
    half = group // 2
    rows_all, wide, deep = GRID
    plane = wide * deep
    mine = lax.rem(me // half + core, 2)
    theirs = 1 - mine
    mate = lax.rem(pair + 1, parts // 2) * 2 + core
    lanes = queries.shape[1] // group
    rows = queries.shape[0]

    def table(index):
        return tables_hbm.at[pl.ds(index * 2 * group, 2 * group)]

    loads = [
        pltpu.make_async_copy(source, target, in_sem.at[index])
        for index, (source, target) in enumerate(
            [(keys, k_buf), (values, v_buf), (queries, q_buf), (cotangent, c_buf), (taps, t_buf), (table(6), pick)]
        )
    ]
    for load in loads:
        load.start()
    barrier = pltpu.get_barrier_semaphore()

    def greet(row, places):
        for place in places:
            pl.semaphore_signal(
                barrier, inc=1, device_id=(part, row * plane + place), device_id_type=MESH
            )

    pl.semaphore_signal(barrier, inc=1, device_id=(mate, me), device_id_type=MESH)
    others(me, greet, (0, rows_all - 1), True)
    pl.semaphore_signal(barrier, inc=1, device_id=(twin, me), device_id_type=MESH)

    tables = [
        pltpu.make_async_copy(source, target, table_sem.at[index])
        for index, (source, target) in enumerate(
            [
                (table(0), forward.at[pl.ds(0, 2 * group)]),
                (table(1), forward.at[pl.ds(2 * group, 2 * group)]),
                (twists_hbm.at[0], twist_cos),
                (twists_hbm.at[1], twist_sin),
                (table(2), inner_forward),
                (table(3), inner_inverse),
                (table(4), inverse.at[0]),
                (table(5), inverse.at[1]),
            ]
        )
    ]
    for load in tables:
        load.start()

    for load in loads:
        load.wait()

    def keep_own(source, target):
        here = pl.ds(0, lanes * rows)
        target[me, :, here] = source[me, :, here]

        @pl.when(core == 0)
        def _():
            here = pl.ds(lanes * rows, 2 * rows)
            target[me, :, here] = source[me, :, here]

    mixed = (k_buf[...].astype(F32) * v_buf[...].astype(F32)).astype(BF16)
    grad_conv = (c_buf[...].astype(F32) * q_buf[...].astype(F32)).astype(BF16)
    spread = pick[...]

    def block(array, index):
        return array[:, index * group : (index + 1) * group]

    pairs = jnp.concatenate(
        [jnp.concatenate([block(mixed, i), block(grad_conv, i)], axis=1) for i in range(lanes)], axis=0
    )
    width = lanes * rows
    there = dot(spread, pairs, (1, 1)).astype(BF16)
    send_there[:, :, pl.ds(0, width)] = there.reshape(group, 2, width)
    tap_rows = t_buf[...]
    tap_pairs = jnp.concatenate(
        [
            jnp.concatenate([block(tap_rows, 0), block(tap_rows, 1)], axis=1),
            jnp.concatenate([block(tap_rows, 2), jnp.zeros((rows, group), BF16)], axis=1),
        ],
        axis=0,
    )
    there = dot(spread, tap_pairs, (1, 1)).astype(BF16)
    send_there[:, :, pl.ds(width, 2 * rows)] = there.reshape(group, 2, 2 * rows)
    keep_own(send_there, recv_there)

    pl.semaphore_wait(barrier, group - 1 + 2)
    pl.semaphore_signal(ready_sem, inc=1, device_id=(mate, me), device_id_type=MESH)

    def remote(source, target, peer_part, peer, index):
        return pltpu.make_async_remote_copy(
            src_ref=source,
            dst_ref=target,
            send_sem=copy_sem.at[index, 0],
            recv_sem=copy_sem.at[index, 1],
            device_id=(peer_part, peer),
            device_id_type=MESH,
        )

    def exchange(source, target, index, steps, own_row):
        def send_whole(row, places):
            @pl.when(row // (rows_all // 2) == mine)
            def _():
                for place in places:
                    peer = row * plane + place
                    remote(source.at[peer], target.at[me], part, peer, index).start()

        def send_part(row, places):
            @pl.when(row // (rows_all // 2) != mine)
            def _():
                here = pl.ds(0, width)
                for place in places:
                    peer = row * plane + place
                    remote(source.at[peer, :, here], target.at[me, :, here], part, peer, index + 1).start()

        others(me, send_whole, steps, own_row)
        others(me, send_part, steps, own_row)

    def wait_bytes(some, sem):
        pltpu.make_async_copy(some, some, sem).wait()

    def finished_whole(buffer, index, side):
        for value in range(2):

            @pl.when(core == value)
            def _():
                wait_bytes(buffer.at[pl.ds(0, half - 1 + value)], copy_sem.at[index, side])

    def finished_parts(buffer, index, side):
        for value in range(2):

            @pl.when(core == value)
            def _():
                wait_bytes(buffer.at[pl.ds(0, half - value), :, pl.ds(0, width)], copy_sem.at[index + 1, side])

    first, rest = pl.ds(0, width), pl.ds(width, 2 * rows)

    def send_first(row, places):
        for place in places:
            peer = row * plane + place
            remote(send_there.at[peer, :, first], recv_there.at[me, :, first], part, peer, 0).start()

    def send_rest(row, places):
        @pl.when(row // (rows_all // 2) == mine)
        def _():
            for place in places:
                peer = row * plane + place
                remote(send_there.at[peer, :, rest], recv_there.at[me, :, rest], part, peer, 1).start()

    others(me, send_first, (0, rows_all - 1), True)
    others(me, send_rest, (0, rows_all - 1), True)

    def finished_first(side):
        wait_bytes(recv_there.at[pl.ds(0, group - 1), :, first], copy_sem.at[0, side])

    def finished_rest(side):
        for value in range(2):

            @pl.when(core == value)
            def _():
                wait_bytes(recv_there.at[pl.ds(0, half - 1 + value), :, rest], copy_sem.at[1, side])


    def to_core(source, target, index):
        return pltpu.make_async_remote_copy(
            src_ref=source,
            dst_ref=target,
            send_sem=core_sem.at[index, 0],
            recv_sem=core_sem.at[index, 1],
            device_id=(twin, me),
            device_id_type=MESH,
        )

    def second(buffer, which):
        return buffer.at[pl.ds(which * half, half), :, pl.ds(width, 2 * rows)]

    for load in tables:
        load.wait()

    def twist(real_part, imag_part, slot):
        rows_here = pl.ds(slot * group, group)
        cosines, sines = twist_cos[...], twist_sin[...]
        turned[rows_here, pl.ds(0, rows)] = (real_part * cosines + imag_part * sines).astype(BF16)
        turned[rows_here, pl.ds(rows, rows)] = (imag_part * cosines - real_part * sines).astype(BF16)

    def stage_forward(buffer, slots, first):
        partial = dot(forward[...], buffer.reshape(2 * group, buffer.shape[2]))
        for offset, (r, j) in enumerate(slots):
            real_part = partial[2 * r * group : (2 * r + 1) * group, j * rows : (j + 1) * rows]
            imag_part = partial[(2 * r + 1) * group : (2 * r + 2) * group, j * rows : (j + 1) * rows]
            twist(real_part, imag_part, first + offset)
        here = pl.ds(first * group, len(slots) * group)
        spectrum[here, :] = dot(turned[here, :], inner_forward[...])

    def halves(slot):
        here = pl.ds(slot * group, group)
        return spectrum[here, pl.ds(0, rows)], spectrum[here, pl.ds(rows, rows)]

    def multiply(left, right, conjugate, slot):
        left_real, left_imag = halves(left)
        right_real, right_imag = halves(right)
        if conjugate:
            right_imag = -right_imag
        here = pl.ds(slot * group, group)
        product[here, pl.ds(0, rows)] = (left_real * right_real - left_imag * right_imag).astype(BF16)
        product[here, pl.ds(rows, rows)] = (left_real * right_imag + left_imag * right_real).astype(BF16)

    def stage_inverse(slots, first, target):
        here = pl.ds(first * group, len(slots) * group)
        back = dot(product[here, :], inner_inverse[...])
        cosines, sines = twist_cos[...], twist_sin[...]
        for offset, (r, j) in enumerate(slots):
            real_part = back[offset * group : (offset + 1) * group, :rows]
            imag_part = back[offset * group : (offset + 1) * group, rows:]
            across = pl.ds(j * rows, rows)
            untwisted[pl.ds(2 * r * group, group), across] = (real_part * cosines - imag_part * sines).astype(BF16)
            untwisted[pl.ds((2 * r + 1) * group, group), across] = (real_part * sines + imag_part * cosines).astype(BF16)
        size = (slots[-1][1] + 1) * rows
        back = (
            dot(inverse[0], untwisted[pl.ds(0, 2 * group), pl.ds(0, size)])
            + dot(inverse[1], untwisted[pl.ds(2 * group, 2 * group), pl.ds(0, size)])
        ).astype(BF16)
        target[:, :, pl.ds(0, size)] = back.reshape(group, 2, size)

    pair_slots = [(r, j) for r in range(2) for j in range(lanes)]
    tap_slots = [(0, 0), (1, 0), (0, 1)]

    finished_first(1)
    stage_forward(recv_there[:, :, first], pair_slots, 0)
    for i in range(lanes):
        multiply(lanes + i, i, True, i)
    untwisted[pl.ds(2 * group, 2 * group), pl.ds(rows, rows)] = jnp.zeros((2 * group, rows), BF16)
    stage_inverse(tap_slots, 0, send_filter)
    filter_copy = to_core(send_filter.at[pl.ds(theirs * half, half)], part_filter, 1)
    filter_copy.start()
    finished_rest(1)
    taps_copy = to_core(second(recv_there, mine), second(recv_there, mine), 0)
    taps_copy.start()

    filter_copy.wait_recv()
    both = send_filter[pl.ds(mine * half, half)].astype(F32) + part_filter[...].astype(F32)
    send_back[pl.ds(mine * half, half), :, rest] = both.astype(BF16)
    pl.semaphore_wait(ready_sem, 1)

    lines = rows_all // 2
    line = lax.rem(me // plane, lines)
    for step in range(lines):
        row = mine * lines + lax.rem(line + step, lines)
        for place in planes(me):
            peer = row * plane + place
            remote(send_back.at[peer, :, rest], cross_filter.at[lax.rem(me, half)], mate, peer, 4).start()

    taps_copy.wait_recv()
    stage_forward(recv_there[:, :, rest], tap_slots, 2 * lanes)
    for i in range(lanes):
        multiply(i, 2 * lanes + i, False, i)
        multiply(lanes + i, 2 * lanes + i, True, lanes + i)
    stage_inverse(pair_slots, 0, send_back)
    keep_own(send_back, recv_back)
    exchange(send_back, recv_back, 2, (0, rows_all - 1), True)

    finished_whole(recv_back, 2, 1)
    wait_bytes(cross_filter, copy_sem.at[4, 1])
    here = second(recv_back, mine)
    here[...] = (here[...].astype(F32) + cross_filter[...].astype(F32)).astype(BF16)
    all_copy = to_core(here, here, 2)
    all_copy.start()
    finished_parts(recv_back, 2, 1)
    flat = recv_back[:, :, first].reshape(2 * group, width)
    for i in range(lanes):
        both = dot(flat[:, i * rows : (i + 1) * rows], spread, (0, 0))
        conv, grad_mixed = both[:, :group], both[:, group:]
        here = pl.ds(i * group, group)
        gated[:, here] = (q_buf[:, here].astype(F32) * conv).astype(BF16)
        grad_queries[:, here] = (c_buf[:, here].astype(F32) * conv).astype(BF16)
        grad_keys[:, here] = (v_buf[:, here].astype(F32) * grad_mixed).astype(BF16)
        grad_values[:, here] = (k_buf[:, here].astype(F32) * grad_mixed).astype(BF16)
    all_copy.wait_recv()
    flat = recv_back[:, :, rest].reshape(2 * group, 2 * rows)
    both = dot(flat[:, :rows], spread, (0, 0))
    filter_first[...] = both[:, :group]
    filter_second[...] = both[:, group:]
    filter_third[...] = dot(flat[:, rows:], spread, (0, 0))[:, :group]
    finished_first(0)
    finished_rest(0)
    finished_whole(send_back, 2, 0)
    finished_parts(send_back, 2, 0)
    wait_bytes(cross_filter, copy_sem.at[4, 0])
    for copy in (taps_copy, filter_copy, all_copy):
        copy.wait_send()


def hand_over(gated, grad_queries, grad_keys, grad_values, first, second, third, *refs):
    *targets, filter_grad, sems = refs
    group = first.shape[1]
    pairs = list(zip((gated, grad_queries, grad_keys, grad_values), targets))
    for index, source in enumerate((first, second, third)):
        pairs.append((source, filter_grad.at[:, pl.ds(index * group, group)]))
    copies = [
        pltpu.make_async_copy(source, target, sems.at[index]) for index, (source, target) in enumerate(pairs)
    ]
    for copy in copies:
        copy.start()
    for copy in copies:
        copy.wait()


def shards(group, parts, queries, keys, values, filter_taps, cotangent):
    rows, channels = filter_taps.shape
    lanes = channels // group
    tables = constant_tables(group, rows)
    vmem = pltpu.VMEM
    local = (rows, channels)
    block = (group, 2, (lanes + 2) * rows)
    single = (group, 2, 2 * rows)
    half = group // 2
    arrays = (queries[0], keys[0], values[0], filter_taps, cotangent[0])
    results = [jax.ShapeDtypeStruct(local, BF16)] * 4 + [jax.ShapeDtypeStruct(local, F32)]
    outs = pl.pallas_call(
        functools.partial(kernel, group, parts),
        out_shape=results[:4] + [jax.ShapeDtypeStruct((rows, group), F32)] * lanes,
        in_specs=[pl.BlockSpec(memory_space=pl.ANY)] * 7,
        out_specs=[pl.BlockSpec(memory_space=vmem)] * (4 + lanes),
        scratch_shapes=[vmem(block, BF16)]
        + [vmem(local, BF16)] * 5
        + [vmem((4 * group, 2 * group), BF16), vmem((2, 2 * group, 2 * group), BF16)]
        + [vmem((2 * group, 2 * group), BF16)] * 3
        + [vmem((group, rows), F32)] * 2
        + [vmem(block, BF16)] * 3
        + [vmem(single, BF16)]
        + [vmem((half,) + single[1:], BF16)] * 2
        + [
            vmem((3 * lanes * group, 2 * rows), BF16),
            vmem((3 * lanes * group, 2 * rows), F32),
            vmem((2 * lanes * group, 2 * rows), BF16),
            vmem((4 * group, lanes * rows), BF16),
            pltpu.SemaphoreType.DMA((6,)),
            pltpu.SemaphoreType.DMA((8,)),
            pltpu.SemaphoreType.DMA((5, 2)),
            pltpu.SemaphoreType.DMA((3, 2)),
            pltpu.SemaphoreType.REGULAR,
        ],
        compiler_params=pltpu.CompilerParams(
            collective_id=0, has_side_effects=True, vmem_limit_bytes=KERNEL_VMEM
        ),
    )(*arrays, *tables)
    outs = pl.pallas_call(
        hand_over,
        out_shape=results,
        in_specs=[pl.BlockSpec(memory_space=vmem)] * (4 + lanes),
        out_specs=[pl.BlockSpec(memory_space=pl.ANY)] * 5,
        scratch_shapes=[pltpu.SemaphoreType.DMA((4 + lanes,))],
        compiler_params=pltpu.CompilerParams(vmem_limit_bytes=16 << 20),
    )(*outs)
    return tuple(out[None] for out in outs[:4]) + (outs[4],)


def solution(mesh):
    spec = P("dp", "ctx", None)
    return jax.shard_map(
        functools.partial(shards, mesh.shape["ctx"], mesh.shape["dp"]),
        mesh=mesh,
        in_specs=(spec, spec, spec, P("ctx", None), spec),
        out_specs=(spec, spec, spec, spec, P("ctx", None)),
        check_vma=False,
    )
```
